256 devices in a mesh: dp: 64 (over y, z, x_lo), mp: 4 (over x_hi, core).
Axes of the slice: x: 4 (x_hi: 2, x_lo: 2; x = x_hi * 2 + x_lo), y: 4, z: 8, core: 2. Of those that a mesh axis runs over, the one named last changes fastest.
Arguments:
- layer_input: bfloat16 [8192, 2560], P('dp'), may hold values from -16 to 16
- gate_weight: bfloat16 [2560, 7168], P('dp', 'mp'), may hold values from -0.125 to 0.125
- up_value: bfloat16 [8192, 7168], P('dp', 'mp'), may hold values from -6 to 6
- hidden_grad: bfloat16 [8192, 7168], P('dp', 'mp'), may hold values from -6 to 6
- sign_bits: int32 [7168], P('mp'), may hold values from 0 to 1
- scale_exponent: int32 [56], P('mp'), may hold values from 0 to 6
Outputs:
- input_grad: bfloat16 [8192, 2560], P(('dp', 'mp'))
- up_grad: bfloat16 [8192, 7168], P('dp', 'mp')
- weight_grad: float32 [2560, 7168], P('dp', 'mp')
The draws below stay inside these ranges and needn't reach their ends.
All inputs are finite; a program needn't handle non-finite values.
Results may differ from the reference program's by a relative error of at most 0.0049.
Values may be sent and summed in bfloat16 or wider, within the bound.
A program may use at most 128 MiB of HBM per device.

```python
import math
import jax
import jax.numpy as jnp
from jax import lax

D = 2560
FF = 7168
TOK_DEV = 128
TOKENS = 8192
NBLOCKS = 56
N_DP = 64


def set_ends(drawn, rng, least, top_value):
    place = [jax.random.randint(jax.random.fold_in(rng, axis), (), 0, length) for axis, length in enumerate(drawn.shape)]
    widest = drawn.shape.index(max(drawn.shape))
    beside = place[:widest] + [(place[widest] + 1) % drawn.shape[widest]] + place[widest + 1:]
    return drawn.at[tuple(place)].set(least).at[tuple(beside)].set(top_value)


def raised(entries, stream_key, source, target, parts, factor):
    def block_of(axis_at):
        return (jnp.arange(entries.shape[axis_at]) // (entries.shape[axis_at] // parts)).reshape((-1,) + (1,) * (entries.ndim - 1 - axis_at))

    one_side = jax.random.permutation(stream_key, parts)[block_of(target)]
    other_side = (block_of(target) + parts // 2) % parts
    return jnp.where((block_of(source) == one_side) | (block_of(source) == other_side), factor * entries, entries)


def levels(key, extent, cuts, low, largest):
    level, own = 1.0, jax.random.fold_in(key, 6)
    for dim, blocks in cuts:
        steps = jnp.exp(jax.random.uniform(jax.random.fold_in(own, dim), (blocks,), jnp.float32, low / len(cuts), largest / len(cuts)))
        level = level * jnp.repeat(steps, extent[dim] // blocks).reshape([-1 if axis == dim else 1 for axis in range(len(extent))])
    return level


def centred(key, shape, width, most, split=(), held_as=jnp.bfloat16):
    gain = levels(key, shape, split, -0.22, 0.18) if split else 1.0
    values = jax.random.normal(key, shape, jnp.float32) * width * gain
    return jnp.minimum(jnp.maximum(values, -most), most).astype(held_as)


def heavy_noise(rng, extent, width, bound, split, heavy, held_as=jnp.bfloat16):
    entries = width * jax.random.normal(rng, extent, jnp.float32)
    if split:
        entries = entries * levels(rng, extent, split, -0.22, 0.18)
    return jnp.clip(raised(entries, jax.random.fold_in(rng, 3), *heavy), -bound, bound).astype(held_as)


def setup_inputs(seed: int = 0) -> dict:
    streams_of = jax.random.split(jax.random.key(seed), 7)
    return {
        "layer_input": heavy_noise(streams_of[0], (TOKENS, D), 1.0, 16.0, ((0, 64),), (0, 1, 64, 4.0)),
        "gate_weight": centred(streams_of[1], (D, FF), D ** -0.5, 0.125, ((0, 64), (1, 4))),
        "up_value": centred(streams_of[2], (TOKENS, FF), 1.0, 6.0, ((0, 64), (1, 4))),
        "hidden_grad": centred(streams_of[3], (TOKENS, FF), 1.0, 6.0, ((0, 64), (1, 4))),
        "sign_bits": set_ends(jax.random.randint(streams_of[4], (FF,), 0, 2), jax.random.fold_in(streams_of[4], 1), 0, 1).astype(jnp.int32),
        "scale_exponent": set_ends(jax.random.randint(streams_of[5], (NBLOCKS,), 0, 7), jax.random.fold_in(streams_of[5], 1), 0, 6).astype(jnp.int32),
    }


def hadamard_matrix():
    rows_index = lax.iota(jnp.int32, 128)
    both_bits = jnp.bitwise_and(rows_index[:, None], rows_index[None, :])
    parity = jnp.zeros((128, 128), jnp.int32)
    for bit_number in range(7):
        parity = parity + jnp.bitwise_and(jnp.right_shift(both_bits, bit_number), 1)
    signs = (1 - 2 * jnp.bitwise_and(parity, 1)).astype(jnp.float32)
    return signs / jnp.float32(math.sqrt(128.0))

def quantize(values, sign_values, hadamard, factors):
    row_total = values.shape[0]
    blocks = (values * sign_values).reshape(row_total, -1, 128)
    turned = jnp.einsum('rbk,kj->rbj', blocks, hadamard, precision=lax.Precision.HIGHEST)
    scaled = jnp.clip(turned * factors[None, :, None], -127.0, 127.0)
    return scaled.reshape(row_total, -1).astype(jnp.bfloat16)

def dequantize(values, sign_values, hadamard, factors):
    row_total = values.shape[0]
    blocks = values.reshape(row_total, -1, 128) / factors[None, :, None]
    turned = jnp.einsum('rbk,kj->rbj', blocks, hadamard, precision=lax.Precision.HIGHEST)
    return turned.reshape(row_total, -1) * sign_values

def reference(layer_input, gate_weight, up_value, hidden_grad, sign_bits, scale_exponent):
    hadamard = hadamard_matrix()
    sign_values = (1 - 2 * sign_bits).astype(jnp.float32)
    factors = jnp.left_shift(jnp.ones_like(scale_exponent), scale_exponent).astype(jnp.float32)
    inputs_split = layer_input.reshape(N_DP, TOK_DEV, D)
    up_split = up_value.reshape(N_DP, TOK_DEV, FF)
    grad_split = hidden_grad.reshape(N_DP, TOK_DEV, FF)

    def replica(running_sum, pieces):
        inputs_here, up_here, grad_here = pieces
        gate_value = jnp.dot(inputs_here, gate_weight, preferred_element_type=jnp.float32)
        sigmoid = jax.nn.sigmoid(gate_value)
        grad_float = grad_here.astype(jnp.float32)
        gate_grad = (grad_float * up_here.astype(jnp.float32) * sigmoid * (1.0 + gate_value * (1.0 - sigmoid))).astype(jnp.bfloat16)
        up_grad = (grad_float * gate_value * sigmoid).astype(jnp.bfloat16)
        input_grad = lax.dot_general(gate_grad, gate_weight, (((1,), (1,)), ((), ())), preferred_element_type=jnp.float32).astype(jnp.bfloat16)
        local_grad = lax.dot_general(inputs_here, gate_grad, (((0,), (0,)), ((), ())), preferred_element_type=jnp.float32)
        quantized = quantize(local_grad, sign_values, hadamard, factors)
        return (running_sum + quantized.astype(jnp.float32), (input_grad, up_grad))
    grad_sum, (input_grads, up_grads) = lax.scan(replica, jnp.zeros((D, FF), jnp.float32), (inputs_split, up_split, grad_split))
    weight_grad = dequantize(grad_sum, sign_values, hadamard, factors)
    return (input_grads.reshape(TOKENS, D), up_grads.reshape(TOKENS, FF), weight_grad)
```

```python
import functools
import math

import jax
import jax.numpy as jnp
from jax import lax
from jax.experimental import pallas as pl
from jax.experimental.pallas import tpu as pltpu
from jax.sharding import PartitionSpec as P

F32 = jnp.float32
BF16 = jnp.bfloat16
MESH = pl.DeviceIdType.MESH
BLOCK = 128
ROOT = 1.0 / math.sqrt(128.0)


def up_to(value, unit):
    return -(-value // unit) * unit


class Dims:
    def __init__(self, ny, nz, tokens, depth, rows, hidden):
        self.ny, self.nz = ny, nz
        self.tokens, self.depth, self.rows, self.hidden = tokens, depth, rows, hidden
        self.half = hidden // 2
        self.blocks = self.half // BLOCK
        self.cols_a = (self.blocks * 3 // 7) * BLOCK
        self.cols_b = self.half - self.cols_a
        self.rb = 2 * rows
        self.yrows = nz * self.rb
        self.pad = up_to(rows, 16)
        cut = up_to(self.rb // 2, 16)
        self.row_subs = ((0, cut), (cut, self.rb - cut))
        quarter = self.yrows // 4
        self.y_subs = tuple((s * quarter, quarter) for s in range(4))


class Ring:
    def __init__(self, me, length, at):
        self.me, self.length, self.half = me, length, length // 2
        self.sides = (at(lax.rem(me + 1, length)), at(lax.rem(me + length - 1, length)))

    def place(self, offset):
        return lax.rem(self.me + offset + self.length, self.length)


class Sends:
    def __init__(self):
        self.open = []

    def start(self, src, dst, send_sem, recv_sem, device):
        copy = pltpu.make_async_remote_copy(
            src_ref=src, dst_ref=dst, send_sem=send_sem, recv_sem=recv_sem,
            device_id=device, device_id_type=MESH,
        )
        copy.start()
        self.open.append(copy)

    def drain(self):
        for copy in self.open:
            copy.wait_send()
        self.open = []


def went(side, sub, count):
    return (sub < (count + 1) // 2) == (side == 0)


class Gather:
    def __init__(self, ring, count, ref, sems, sends):
        self.ring, self.count, self.ref = ring, count, ref
        self.send_sems, self.recv_sems = sems
        self.sends = sends

    def wait_one(self, side, step, sub):
        origin = self.ring.place(-step if side == 0 else step)
        here = self.ref(origin, sub)
        pltpu.make_async_remote_copy(
            src_ref=here, dst_ref=here,
            send_sem=self.send_sems.at[side, step - 1, sub],
            recv_sem=self.recv_sems.at[side, step - 1, sub],
            device_id=self.ring.sides[side], device_id_type=MESH,
        ).wait_recv()

    def send(self, step):
        last = step == self.ring.half
        for sub in range(self.count):
            for side in (0, 1):
                if step > 1:
                    self.wait_one(side, step - 1, sub)
                if last and not went(side, sub, self.count):
                    continue
                origin = self.ring.place(-(step - 1) if side == 0 else step - 1)
                here = self.ref(origin, sub)
                self.sends.start(
                    here, here,
                    self.send_sems.at[side, step - 1, sub],
                    self.recv_sems.at[side, step - 1, sub],
                    self.ring.sides[side],
                )

    def finish(self):
        for sub in range(self.count):
            for side in (0, 1):
                if went(side, sub, self.count):
                    self.wait_one(side, self.ring.half, sub)


class Scatter:
    def __init__(self, ring, count, own, out, landing, sems, sends):
        self.ring, self.count, self.own, self.out, self.landing = ring, count, own, out, landing
        self.send_sems, self.recv_sems = sems
        self.sends = sends

    def arrived(self, side, step, sub):
        return step < 1 or step > 1 or went(side, sub, self.count)

    def take(self, side, step, sub):
        here = self.landing(side, step - 1, sub)
        pltpu.make_async_remote_copy(
            src_ref=here, dst_ref=here,
            send_sem=self.send_sems.at[side, step - 1, sub],
            recv_sem=self.recv_sems.at[side, step - 1, sub],
            device_id=self.ring.sides[side], device_id_type=MESH,
        ).wait_recv()
        return here[...].astype(F32)

    def send(self, step):
        far = self.ring.half + 1 - step
        for sub in range(self.count):
            for side in (0, 1):
                if step == 1 and not went(side, sub, self.count):
                    continue
                target = self.ring.place(far if side == 0 else -far)
                total = self.own(target, sub)[...]
                if step > 1 and self.arrived(side, step - 1, sub):
                    total = total + self.take(side, step - 1, sub)
                out = self.out(target, sub)
                out[...] = total.astype(BF16)
                self.sends.start(
                    out, self.landing(side, step - 1, sub),
                    self.send_sems.at[side, step - 1, sub],
                    self.recv_sems.at[side, step - 1, sub],
                    self.ring.sides[side],
                )

    def finish(self):
        for sub in range(self.count):
            mine = self.own(self.ring.me, sub)
            total = mine[...]
            for side in (0, 1):
                if self.arrived(side, self.ring.half, sub):
                    total = total + self.take(side, self.ring.half, sub)
            mine[...] = total


def hadamard_signs():
    both = jnp.bitwise_and(
        lax.broadcasted_iota(jnp.int32, (BLOCK, BLOCK), 0),
        lax.broadcasted_iota(jnp.int32, (BLOCK, BLOCK), 1),
    )
    for shift in (4, 2, 1):
        both = jnp.bitwise_xor(both, jnp.right_shift(both, shift))
    return (1 - 2 * jnp.bitwise_and(both, 1)).astype(F32).astype(BF16)


def kernel(
    dims,
    x_ref, w_ref, up_ref, hg_ref, bits_ref, exp_ref,
    ig_ref, ug_ref, wg_ref,
    x2, xt, hg2, up2, upg2, wsend, wrecv, wa, wb, g_a, g_b, turned, had,
    sa, sb, oa, ob, la_z, la_y, lb_y, lb_z,
    part, core_out, core_in, chip_out, chip_in,
    x_sems, core_sems, ip_sems, fin_sems, local_sem,
    ga_y_s, ga_y_r, ga_z_s, ga_z_r, gb_z_s, gb_z_r, gb_y_s, gb_y_r,
    ra_z_s, ra_z_r, ra_y_s, ra_y_r, rb_y_s, rb_y_r, rb_z_s, rb_z_r,
):
    d = dims
    t, hf, rb = d.tokens, d.half, d.rb
    dp, mp = lax.axis_index("dp"), lax.axis_index("mp")
    xl, yz = lax.rem(dp, 2), lax.div(dp, 2)
    z, y = lax.rem(yz, d.nz), lax.div(yz, d.nz)
    core, xh = lax.rem(mp, 2), lax.div(mp, 2)

    def device(y=y, z=z, xl=xl, xh=xh, core=core):
        return {"dp": (y * d.nz + z) * 2 + xl, "mp": xh * 2 + core}

    ring_y = Ring(y, d.ny, lambda place: device(y=place))
    ring_z = Ring(z, d.nz, lambda place: device(z=place))
    partner, sibling = device(xl=1 - xl), device(core=1 - core)
    across = (partner, device(xh=1 - xh), device(xl=1 - xl, xh=1 - xh))

    barrier = pltpu.get_barrier_semaphore()
    others = ring_y.sides + ring_z.sides + across + (sibling,)
    for other in others:
        pl.semaphore_signal(barrier, inc=1, device_id=other, device_id_type=MESH)

    sends = Sends()
    here = pl.ds(pl.multiple_of(xl * hf, BLOCK), hf)
    there = pl.ds(pl.multiple_of((1 - xl) * hf, BLOCK), hf)

    def padded(columns):
        rows = w_ref[:, columns].astype(F32)
        if d.pad == d.rows:
            return rows
        return jnp.concatenate([rows, jnp.zeros((d.pad - d.rows, hf), F32)], axis=0)

    wsend[...] = padded(there).astype(BF16)
    pl.semaphore_wait(barrier, len(others))

    sends.start(wsend, wrecv, x_sems.at[0, 0], x_sems.at[1, 0], partner)
    x_rows = pl.ds(pl.multiple_of(core * (t // 2), 16), t // 2)
    sends.start(x_ref.at[x_rows, :], x2.at[xl, x_rows, :], x_sems.at[0, 1], x_sems.at[1, 1], partner)
    sends.start(hg_ref.at[:, there], hg2.at[xl], x_sems.at[0, 2], x_sems.at[1, 2], partner)
    sends.start(up_ref.at[:, there], up2.at[xl], x_sems.at[0, 3], x_sems.at[1, 3], partner)
    own_x = pltpu.make_async_copy(x_ref, x2.at[xl], local_sem)
    own_x.start()

    def landed(ref, index):
        pltpu.make_async_remote_copy(
            src_ref=ref, dst_ref=ref, send_sem=x_sems.at[0, index], recv_sem=x_sems.at[1, index],
            device_id=partner, device_id_type=MESH,
        ).wait_recv()

    z_rows = lambda place: pl.multiple_of(place * rb, 16)
    ra = lambda ref: lambda place, sub: ref.at[place, pl.ds(z_rows(z) + d.row_subs[sub][0], d.row_subs[sub][1]), :]
    rz = lambda ref: lambda place, sub: ref.at[sub, pl.ds(z_rows(place), rb), :]
    rbz = lambda ref: lambda place, sub: ref.at[y, pl.ds(z_rows(place) + d.row_subs[sub][0], d.row_subs[sub][1]), :]
    rby = lambda ref: lambda place, sub: ref.at[place, pl.ds(d.y_subs[sub][0], d.y_subs[sub][1]), :]

    gather_a_y = Gather(ring_y, 2, ra(wa), (ga_y_s, ga_y_r), sends)
    gather_a_z = Gather(ring_z, d.ny, rz(wa), (ga_z_s, ga_z_r), sends)
    gather_b_z = Gather(ring_z, 2, rbz(wb), (gb_z_s, gb_z_r), sends)
    gather_b_y = Gather(ring_y, 4, rby(wb), (gb_y_s, gb_y_r), sends)

    landed(wrecv, 0)
    own_rows = w_ref[:, here].astype(F32)
    other_rows = wrecv[...].astype(F32)[: d.rows]
    low = jnp.where(xl == 0, own_rows, other_rows)
    high = jnp.where(xl == 0, other_rows, own_rows)
    rows = jnp.concatenate([low, high], axis=0).astype(BF16)
    wa[y, pl.ds(z_rows(z), rb), :] = rows[:, : d.cols_a]
    wb[y, pl.ds(z_rows(z), rb), :] = rows[:, d.cols_a :]

    gather_a_y.send(1)
    gather_b_z.send(1)
    had[...] = hadamard_signs()
    for step in range(2, d.ny // 2 + 1):
        gather_a_y.send(step)
    gather_a_y.finish()
    gather_a_z.send(1)
    for step in range(2, d.nz // 2 + 1):
        gather_b_z.send(step)
    gather_b_z.finish()
    gather_b_y.send(1)

    own_x.wait()
    theirs = x2.at[1 - xl, x_rows, :]
    landed(theirs, 1)
    sends.start(theirs, theirs, core_sems.at[0, 0], core_sems.at[1, 0], sibling)

    per_y = d.yrows // BLOCK

    def turn(replica):
        @pl.loop(0, d.depth // BLOCK)
        def _(chunk):
            tile = x2[replica, :, pl.ds(pl.multiple_of(chunk * BLOCK, BLOCK), BLOCK)]
            tile = tile.astype(F32).T.astype(BF16)
            at = pl.ds(pl.multiple_of(lax.rem(chunk, per_y) * BLOCK, BLOCK), BLOCK)
            xt[replica, lax.div(chunk, per_y), at, 0:t] = tile
            xt[replica, lax.div(chunk, per_y), at, t : 2 * t] = tile

    turn(xl)
    for step in range(2, d.nz // 2 + 1):
        gather_a_z.send(step)
        if step == 2:
            other_x = pl.ds(pl.multiple_of((1 - core) * (t // 2), 16), t // 2)
            rest = x2.at[1 - xl, other_x, :]
            pltpu.make_async_remote_copy(
                src_ref=rest, dst_ref=rest, send_sem=core_sems.at[0, 0], recv_sem=core_sems.at[1, 0],
                device_id=sibling, device_id_type=MESH,
            ).wait_recv()
    turn(1 - xl)
    for step in range(2, d.ny // 2 + 1):
        gather_b_y.send(step)
    landed(hg2.at[1 - xl], 2)
    landed(up2.at[1 - xl], 3)
    hg2[xl] = hg_ref[:, here]
    up2[xl] = up_ref[:, here]
    gather_a_z.finish()
    gather_b_y.finish()

    def scale_of(block):
        return jnp.left_shift(1, exp_ref[xl * d.blocks + block]).astype(F32)

    def inverse_of(block):
        return jnp.right_shift(64, exp_ref[xl * d.blocks + block]).astype(F32) * (1.0 / 64.0)

    def signs_of(block):
        bits = bits_ref[:, pl.ds(pl.multiple_of(xl * hf + block * BLOCK, BLOCK), BLOCK)]
        return (1 - 2 * bits).astype(F32)

    def gate_tile(w_part, g_part, base, start, width):
        columns = slice(start, start + width)
        gate = jnp.zeros((2 * t, width), F32)
        for place in range(d.ny):
            at = slice(place * d.yrows, (place + 1) * d.yrows)
            gate = gate + jnp.dot(
                x2[:, :, at].reshape(2 * t, d.yrows), w_part[place, :, columns],
                preferred_element_type=F32,
            )
        at = slice(base + start, base + start + width)
        grad = hg2[:, :, at].reshape(2 * t, width).astype(F32)
        up = up2[:, :, at].reshape(2 * t, width).astype(F32)
        s = jax.nn.sigmoid(gate)
        gate_grad = (grad * up * s * (1.0 + gate * (1.0 - s))).astype(BF16)
        g_part[:, columns] = gate_grad
        upg2[:, :, at] = (grad * gate * s).astype(BF16).reshape(2, t, width)
        for piece in range(width // BLOCK):
            block = (base + start) // BLOCK + piece
            flipped = gate_grad[:, piece * BLOCK : (piece + 1) * BLOCK].astype(F32) * signs_of(block)
            rotated = jnp.dot(flipped.astype(BF16), had[...], preferred_element_type=F32)
            rotated = rotated * (scale_of(block) * ROOT)
            top = rotated.astype(BF16)
            rest = (rotated - top.astype(F32)).astype(BF16)
            put = slice(block * BLOCK, (block + 1) * BLOCK)
            for replica in (0, 1):
                mine = slice(replica * t, (replica + 1) * t)
                turned[replica, 0:t, put] = top[mine]
                turned[replica, t : 2 * t, put] = rest[mine]

    for start in range(0, d.cols_b, 2 * BLOCK):
        gate_tile(wb, g_b, d.cols_a, start, min(2 * BLOCK, d.cols_b - start))
    for start in range(0, d.cols_a, 2 * BLOCK):
        gate_tile(wa, g_a, 0, start, min(2 * BLOCK, d.cols_a - start))

    sends.start(upg2.at[1 - xl], ug_ref.at[:, here], x_sems.at[0, 4], x_sems.at[1, 4], partner)
    ug_ref[:, here] = upg2[xl]

    def quantized(lhs, replica, columns):
        value = jnp.dot(lhs, turned[replica, :, columns], preferred_element_type=F32)
        return jnp.clip(value, -127.0, 127.0).astype(BF16).astype(F32)

    def order(j, ring):
        return ring.place((ring.half - lax.div(j + 1, 2)) * (2 * lax.rem(j, 2) - 1))

    def grads_a(low, high):
        @pl.loop(low, high)
        def _(j):
            at = pl.ds(z_rows(order(j, ring_z)), rb)
            total = 0.0
            for replica in (0, 1):
                lhs = xt[replica, :, at, :].reshape(d.ny * rb, 2 * t)
                total = total + quantized(lhs, replica, slice(0, d.cols_a))
            sa[:, at, :] = total.reshape(d.ny, rb, d.cols_a)

    def grads_b(low, high):
        @pl.loop(low * 2, high * 2)
        def _(j):
            place = order(lax.div(j, 2), ring_y)
            at = pl.ds(pl.multiple_of(lax.rem(j, 2) * (d.yrows // 2), 16), d.yrows // 2)
            total = 0.0
            for replica in (0, 1):
                total = total + quantized(xt[replica, place, at, :], replica, slice(d.cols_a, hf))
            sb[place, at, :] = total

    at_sub = lambda ref: lambda side, step, sub: ref.at[side, step, sub]
    at_rows = lambda ref: lambda side, step, sub: ref.at[side, step, pl.ds(d.row_subs[sub][0], d.row_subs[sub][1]), :]
    at_y = lambda ref: lambda side, step, sub: ref.at[side, step, pl.ds(d.y_subs[sub][0], d.y_subs[sub][1]), :]
    scatter_a_z = Scatter(ring_z, d.ny, rz(sa), rz(oa), at_sub(la_z), (ra_z_s, ra_z_r), sends)
    scatter_a_y = Scatter(ring_y, 2, ra(sa), ra(oa), at_rows(la_y), (ra_y_s, ra_y_r), sends)
    scatter_b_y = Scatter(ring_y, 4, rby(sb), rby(ob), at_y(lb_y), (rb_y_s, rb_y_r), sends)
    scatter_b_z = Scatter(ring_z, 2, rbz(sb), rbz(ob), at_rows(lb_z), (rb_z_s, rb_z_r), sends)

    grads_b(0, 1)
    scatter_b_y.send(1)
    grads_a(0, 1)
    scatter_a_z.send(1)
    grads_a(1, d.nz)
    grads_b(1, d.ny)

    def partial_tile(place):
        total = 0.0
        for w_part, g_part in ((wa, g_a), (wb, g_b)):
            total = total + lax.dot_general(
                g_part[...], w_part[place], (((1,), (1,)), ((), ())), preferred_element_type=F32
            )
        return total.reshape(8, t // 4, d.yrows)

    @pl.loop(0, d.ny)
    def _(place):
        part[:, :, pl.ds(pl.multiple_of(place * d.yrows, BLOCK), d.yrows)] = partial_tile(place)

    @pl.loop(0, 4)
    def _(q):
        core_out[q] = part[2 * q + 1 - core].astype(BF16)

    sends.start(core_out, core_in, core_sems.at[0, 1], core_sems.at[1, 1], sibling)

    def x_stage():
        pltpu.make_async_remote_copy(
            src_ref=core_in, dst_ref=core_in, send_sem=core_sems.at[0, 1], recv_sem=core_sems.at[1, 1],
            device_id=sibling, device_id_type=MESH,
        ).wait_recv()
        places = (
            (1 - xl) * 2 + xh, xl * 2 + (1 - xh), (1 - xl) * 2 + (1 - xh),
        )
        for index, q in enumerate(places):
            chip_out[index] = (part[2 * q + core] + core_in[q].astype(F32)).astype(BF16)
            sends.start(
                chip_out.at[index], chip_in.at[index], ip_sems.at[0, index], ip_sems.at[1, index], across[index]
            )

    for step in range(2, d.nz // 2 + 1):
        scatter_a_z.send(step)
        if step == 2:
            x_stage()
    for step in range(2, d.ny // 2 + 1):
        scatter_b_y.send(step)
    scatter_a_z.finish()
    scatter_a_y.send(1)
    scatter_b_y.finish()
    scatter_b_z.send(1)
    for step in range(2, d.ny // 2 + 1):
        scatter_a_y.send(step)
    for step in range(2, d.nz // 2 + 1):
        scatter_b_z.send(step)

    def restore(source, base, columns):
        for piece in range(columns // BLOCK):
            block = base // BLOCK + piece
            value = source[y, pl.ds(z_rows(z), rb), piece * BLOCK : (piece + 1) * BLOCK] * inverse_of(block)
            total = 0.0
            for _ in range(3):
                top = value.astype(BF16)
                total = total + jnp.dot(top, had[...], preferred_element_type=F32)
                value = value - top.astype(F32)
            source[y, pl.ds(z_rows(z), rb), piece * BLOCK : (piece + 1) * BLOCK] = total * (signs_of(block) * ROOT)
        near = pl.ds(pl.multiple_of(z_rows(z) + xl * d.rows, 8), d.rows)
        far = pl.ds(pl.multiple_of(z_rows(z) + (1 - xl) * d.rows, 8), d.rows)
        columns_at = pl.ds(pl.multiple_of(xl * hf + base, BLOCK), columns)
        which = 0 if base == 0 else 1
        sends.start(
            source.at[y, far, :], wg_ref.at[:, columns_at], fin_sems.at[0, which], fin_sems.at[1, which], partner
        )
        wg_ref[:, columns_at] = source[y, near, :]

    scatter_a_y.finish()
    restore(sa, 0, d.cols_a)
    scatter_b_z.finish()
    restore(sb, d.cols_a, d.cols_b)

    mine = xl * 2 + xh
    total = part[2 * mine + core] + core_in[mine].astype(F32)
    for index in range(3):
        slot = chip_in.at[index]
        pltpu.make_async_remote_copy(
            src_ref=slot, dst_ref=slot, send_sem=ip_sems.at[0, index], recv_sem=ip_sems.at[1, index],
            device_id=across[index], device_id_type=MESH,
        ).wait_recv()
        total = total + slot[...].astype(F32)
    ig_ref[...] = total.astype(BF16)

    landed(ug_ref.at[:, there], 4)
    for which, base, columns in ((0, 0, d.cols_a), (1, d.cols_a, d.cols_b)):
        slot = wg_ref.at[:, pl.ds(pl.multiple_of((1 - xl) * hf + base, BLOCK), columns)]
        pltpu.make_async_remote_copy(
            src_ref=slot, dst_ref=slot, send_sem=fin_sems.at[0, which], recv_sem=fin_sems.at[1, which],
            device_id=partner, device_id_type=MESH,
        ).wait_recv()
    sends.drain()


def local(ny, nz, layer_input, gate_weight, up_value, hidden_grad, sign_bits, scale_exponent):
    tokens, depth = layer_input.shape
    rows, hidden = gate_weight.shape
    d = Dims(ny, nz, tokens, depth, rows, hidden)
    t, hf, rb = d.tokens, d.half, d.rb
    hy, hz = ny // 2, nz // 2
    vm = lambda shape, dtype: pltpu.VMEM(shape, dtype)
    sem = lambda *shape: pltpu.SemaphoreType.DMA(shape)
    pair = lambda *shape: [sem(*shape), sem(*shape)]
    scratch = [
        vm((2, t, depth), BF16), vm((2, ny, d.yrows, 2 * t), BF16),
        vm((2, t, hf), BF16), vm((2, t, hf), BF16), vm((2, t, hf), BF16),
        vm((d.pad, hf), BF16), vm((d.pad, hf), BF16),
        vm((ny, d.yrows, d.cols_a), BF16), vm((ny, d.yrows, d.cols_b), BF16),
        vm((2 * t, d.cols_a), BF16), vm((2 * t, d.cols_b), BF16),
        vm((2, 2 * t, hf), BF16), vm((BLOCK, BLOCK), BF16),
        vm((ny, d.yrows, d.cols_a), F32), vm((ny, d.yrows, d.cols_b), F32),
        vm((ny, d.yrows, d.cols_a), BF16), vm((ny, d.yrows, d.cols_b), BF16),
        vm((2, hz, ny, rb, d.cols_a), BF16), vm((2, hy, rb, d.cols_a), BF16),
        vm((2, hy, d.yrows, d.cols_b), BF16), vm((2, hz, rb, d.cols_b), BF16),
        vm((8, t // 4, depth), F32), vm((4, t // 4, depth), BF16), vm((4, t // 4, depth), BF16),
        vm((3, t // 4, depth), BF16), vm((3, t // 4, depth), BF16),
        sem(2, 5), sem(2, 2), sem(2, 3), sem(2, 2), pltpu.SemaphoreType.DMA,
        *pair(2, hy, 2), *pair(2, hz, ny), *pair(2, hz, 2), *pair(2, hy, 4),
        *pair(2, hz, ny), *pair(2, hy, 2), *pair(2, hy, 4), *pair(2, hz, 2),
    ]
    whole = pl.BlockSpec(memory_space=pltpu.VMEM)
    return pl.pallas_call(
        functools.partial(kernel, d),
        out_shape=(
            jax.ShapeDtypeStruct((t // 4, depth), BF16),
            jax.ShapeDtypeStruct((t, hidden), BF16),
            jax.ShapeDtypeStruct((rows, hidden), F32),
        ),
        in_specs=[whole] * 5 + [pl.BlockSpec(memory_space=pltpu.SMEM)],
        out_specs=(whole,) * 3,
        scratch_shapes=scratch,
        compiler_params=pltpu.CompilerParams(
            collective_id=0, has_side_effects=True, vmem_limit_bytes=56 * 1024 * 1024
        ),
        name="gate_backward",
    )(layer_input, gate_weight, up_value, hidden_grad, sign_bits.reshape(1, hidden), scale_exponent)


def build(mesh, ny, nz):
    return jax.shard_map(
        functools.partial(local, ny, nz),
        mesh=mesh,
        in_specs=(P("dp", None), P("dp", "mp"), P("dp", "mp"), P("dp", "mp"), P("mp"), P("mp")),
        out_specs=(P(("dp", "mp"), None), P("dp", "mp"), P("dp", "mp")),
        check_vma=False,
    )


def solution(mesh):
    return build(mesh, 4, 8)
```

```python
import functools
import math

import jax
import jax.numpy as jnp
from jax import lax
from jax.experimental import pallas as pl
from jax.experimental.pallas import tpu as pltpu
from jax.sharding import PartitionSpec as P

F32 = jnp.float32
BF16 = jnp.bfloat16
MESH = pl.DeviceIdType.MESH
BLOCK = 128
ROOT = 1.0 / math.sqrt(128.0)


def up_to(value, unit):
    return -(-value // unit) * unit


class Dims:
    def __init__(self, ny, nz, tokens, depth, rows, hidden):
        self.ny, self.nz = ny, nz
        self.tokens, self.depth, self.rows, self.hidden = tokens, depth, rows, hidden
        self.half = hidden // 2
        self.blocks = self.half // BLOCK
        self.cols_a = (self.blocks * 3 // 7) * BLOCK
        self.cols_b = self.half - self.cols_a
        self.rb = 2 * rows
        self.yrows = nz * self.rb
        self.pad = up_to(rows, 16)
        cut = up_to(self.rb // 2, 16)
        self.row_subs = ((0, cut), (cut, self.rb - cut))


class Ring:
    def __init__(self, me, length, at):
        self.me, self.length, self.half = me, length, length // 2
        self.sides = (at(lax.rem(me + 1, length)), at(lax.rem(me + length - 1, length)))

    def place(self, offset):
        return lax.rem(self.me + offset + self.length, self.length)


class Sends:
    def __init__(self):
        self.open = []

    def start(self, src, dst, send_sem, recv_sem, device):
        copy = pltpu.make_async_remote_copy(
            src_ref=src, dst_ref=dst, send_sem=send_sem, recv_sem=recv_sem,
            device_id=device, device_id_type=MESH,
        )
        copy.start()
        self.open.append(copy)

    def drain(self):
        for copy in self.open:
            copy.wait_send()
        self.open = []


def went(side, sub, count):
    return sub % 2 == side


def nearest_first(length):
    half = length // 2
    return [0] + [sign * hops for hops in range(1, half) for sign in (1, -1)] + [half]


class Gather:
    def __init__(self, ring, count, ref, sems, sends):
        self.ring, self.count, self.ref = ring, count, ref
        self.send_sems, self.recv_sems = sems
        self.sends = sends

    def wait_one(self, side, step, sub):
        origin = self.ring.place(-step if side == 0 else step)
        here = self.ref(origin, sub)
        pltpu.make_async_remote_copy(
            src_ref=here, dst_ref=here,
            send_sem=self.send_sems.at[side, step - 1, sub],
            recv_sem=self.recv_sems.at[side, step - 1, sub],
            device_id=self.ring.sides[side], device_id_type=MESH,
        ).wait_recv()

    def send(self, step, subs=None):
        last = step == self.ring.half
        for sub in range(self.count) if subs is None else subs:
            for side in (0, 1):
                if step > 1:
                    self.wait_one(side, step - 1, sub)
                if last and not went(side, sub, self.count):
                    continue
                origin = self.ring.place(-(step - 1) if side == 0 else step - 1)
                here = self.ref(origin, sub)
                self.sends.start(
                    here, here,
                    self.send_sems.at[side, step - 1, sub],
                    self.recv_sems.at[side, step - 1, sub],
                    self.ring.sides[side],
                )

    def finish(self):
        for sub in range(self.count):
            for side in (0, 1):
                if went(side, sub, self.count):
                    self.wait_one(side, self.ring.half, sub)


class Scatter:
    def __init__(self, ring, count, own, out, landing, sems, sends):
        self.ring, self.count, self.own, self.out, self.landing = ring, count, own, out, landing
        self.send_sems, self.recv_sems = sems
        self.sends = sends

    def arrived(self, side, step, sub):
        return step < 1 or step > 1 or went(side, sub, self.count)

    def take(self, side, step, sub):
        here = self.landing(side, step - 1, sub)
        pltpu.make_async_remote_copy(
            src_ref=here, dst_ref=here,
            send_sem=self.send_sems.at[side, step - 1, sub],
            recv_sem=self.recv_sems.at[side, step - 1, sub],
            device_id=self.ring.sides[side], device_id_type=MESH,
        ).wait_recv()
        return here[...].astype(F32)

    def send(self, step, subs=None):
        far = self.ring.half + 1 - step
        for sub in range(self.count) if subs is None else subs:
            for side in (0, 1):
                if step == 1 and not went(side, sub, self.count):
                    continue
                target = self.ring.place(far if side == 0 else -far)
                total = self.own(target, sub)[...]
                if step > 1 and self.arrived(side, step - 1, sub):
                    total = total + self.take(side, step - 1, sub)
                out = self.out(target, sub)
                out[...] = total.astype(BF16)
                self.sends.start(
                    out, self.landing(side, step - 1, sub),
                    self.send_sems.at[side, step - 1, sub],
                    self.recv_sems.at[side, step - 1, sub],
                    self.ring.sides[side],
                )

    def finish(self, subs=None):
        for sub in range(self.count) if subs is None else subs:
            mine = self.own(self.ring.me, sub)
            total = mine[...]
            for side in (0, 1):
                if self.arrived(side, self.ring.half, sub):
                    total = total + self.take(side, self.ring.half, sub)
            mine[...] = total


def hadamard_signs():
    both = jnp.bitwise_and(
        lax.broadcasted_iota(jnp.int32, (BLOCK, BLOCK), 0),
        lax.broadcasted_iota(jnp.int32, (BLOCK, BLOCK), 1),
    )
    for shift in (4, 2, 1):
        both = jnp.bitwise_xor(both, jnp.right_shift(both, shift))
    return (1 - 2 * jnp.bitwise_and(both, 1)).astype(F32).astype(BF16)


def kernel(
    dims,
    x_ref, w_ref, up_ref, hg_ref, bits_ref, exp_ref,
    ig_ref, ug_ref, wg_ref,
    w_own, bits, x2, xt, hg2, up2, upg2, wsend, wrecv, wa, wb, g_a, g_b, turned, had,
    sa, sb, oa, ob, la_z, la_y, lb_y, lb_z,
    part, core_out, core_in, chip_out, chip_in,
    x_sems, core_sems, ip_sems, fin_sems, local_sems,
    ga_y_s, ga_y_r, ga_z_s, ga_z_r, gb_z_s, gb_z_r, gb_y_s, gb_y_r,
    ra_z_s, ra_z_r, ra_y_s, ra_y_r, rb_y_s, rb_y_r, rb_z_s, rb_z_r,
):
    d = dims
    t, hf, rb = d.tokens, d.half, d.rb
    dp, mp = lax.axis_index("dp"), lax.axis_index("mp")
    xl, yz = lax.rem(dp, 2), lax.div(dp, 2)
    z, y = lax.rem(yz, d.nz), lax.div(yz, d.nz)
    core, xh = lax.rem(mp, 2), lax.div(mp, 2)

    def device(y=y, z=z, xl=xl, xh=xh, core=core):
        return {"dp": (y * d.nz + z) * 2 + xl, "mp": xh * 2 + core}

    ring_y = Ring(y, d.ny, lambda place: device(y=place))
    ring_z = Ring(z, d.nz, lambda place: device(z=place))
    partner, sibling = device(xl=1 - xl), device(core=1 - core)
    across = (partner, device(xh=1 - xh), device(xl=1 - xl, xh=1 - xh))

    barrier = pltpu.get_barrier_semaphore()
    others = ring_y.sides + ring_z.sides + across + (sibling,)
    for other in others:
        pl.semaphore_signal(barrier, inc=1, device_id=other, device_id_type=MESH)

    sends = Sends()
    loads = []

    def load(src, dst):
        copy = pltpu.make_async_copy(src, dst, local_sems.at[len(loads)])
        copy.start()
        loads.append(copy)

    here = pl.ds(pl.multiple_of(xl * hf, BLOCK), hf)
    there = pl.ds(pl.multiple_of((1 - xl) * hf, BLOCK), hf)

    load(w_ref, w_own)
    load(x_ref, x2.at[xl])
    load(hg_ref.at[:, here], hg2.at[xl])
    load(up_ref.at[:, here], up2.at[xl])
    for block in range(d.blocks):
        at = pl.ds(pl.multiple_of(xl * hf + block * BLOCK, BLOCK), BLOCK)
        load(bits_ref.at[at], bits.at[block])

    def padded(columns):
        rows = w_own[:, columns].astype(F32)
        if d.pad == d.rows:
            return rows
        return jnp.concatenate([rows, jnp.zeros((d.pad - d.rows, hf), F32)], axis=0)

    loads[0].wait()
    wsend[...] = padded(there).astype(BF16)
    pl.semaphore_wait(barrier, len(others))

    sends.start(wsend, wrecv, x_sems.at[0, 0], x_sems.at[1, 0], partner)
    x_rows = pl.ds(pl.multiple_of(core * (t // 2), 16), t // 2)
    sends.start(x_ref.at[x_rows, :], x2.at[xl, x_rows, :], x_sems.at[0, 1], x_sems.at[1, 1], partner)
    sends.start(hg_ref.at[:, there], hg2.at[xl], x_sems.at[0, 2], x_sems.at[1, 2], partner)
    sends.start(up_ref.at[:, there], up2.at[xl], x_sems.at[0, 3], x_sems.at[1, 3], partner)

    def landed(ref, index):
        pltpu.make_async_remote_copy(
            src_ref=ref, dst_ref=ref, send_sem=x_sems.at[0, index], recv_sem=x_sems.at[1, index],
            device_id=partner, device_id_type=MESH,
        ).wait_recv()

    z_rows = lambda place: pl.multiple_of(place * rb, 16)
    near_y, near_z = nearest_first(d.ny), nearest_first(d.nz)
    far_y, far_z = near_y[::-1], near_z[::-1]
    part_of = lambda place, sub: pl.ds(z_rows(place) + d.row_subs[sub][0], d.row_subs[sub][1])

    def along_y(ref):
        return lambda place, sub: ref.at[place, part_of(z, sub), :]

    def along_z(ref):
        return lambda place, sub: ref.at[y, part_of(place, sub), :]

    def along_z_of_y(ref, offsets):
        return lambda place, sub: ref.at[ring_y.place(offsets[sub]), pl.ds(z_rows(place), rb), :]

    def along_y_of_z(ref, offsets):
        return lambda place, sub: ref.at[place, pl.ds(z_rows(ring_z.place(offsets[sub])), rb), :]

    gather_a_y = Gather(ring_y, 2, along_y(wa), (ga_y_s, ga_y_r), sends)
    gather_a_z = Gather(ring_z, d.ny, along_z_of_y(wa, near_y), (ga_z_s, ga_z_r), sends)
    gather_b_z = Gather(ring_z, 2, along_z(wb), (gb_z_s, gb_z_r), sends)
    gather_b_y = Gather(ring_y, d.nz, along_y_of_z(wb, near_z), (gb_y_s, gb_y_r), sends)

    landed(wrecv, 0)
    own_rows = w_own[:, here].astype(F32)
    other_rows = wrecv[...].astype(F32)[: d.rows]
    low = jnp.where(xl == 0, own_rows, other_rows)
    high = jnp.where(xl == 0, other_rows, own_rows)
    rows = jnp.concatenate([low, high], axis=0).astype(BF16)
    wa[y, pl.ds(z_rows(z), rb), :] = rows[:, : d.cols_a]
    wb[y, pl.ds(z_rows(z), rb), :] = rows[:, d.cols_a :]

    per_y = d.yrows // BLOCK

    def turn(replica, place):
        @pl.loop(0, per_y)
        def _(chunk):
            at = pl.ds(pl.multiple_of(chunk * BLOCK, BLOCK), BLOCK)
            tile = x2[replica, :, pl.ds(pl.multiple_of(place * d.yrows + chunk * BLOCK, BLOCK), BLOCK)]
            tile = tile.astype(F32).T.astype(BF16)
            xt[replica, place, at, 0:t] = tile
            xt[replica, place, at, t : 2 * t] = tile

    gather_b_z.send(1)
    gather_a_y.send(1)
    gather_b_y.send(1, [0])
    gather_a_z.send(1, [0])
    had[...] = hadamard_signs()
    gather_b_z.send(2)
    gather_b_y.send(1, [1, 2])
    gather_a_y.send(2)
    gather_a_z.send(1, [1, 2])
    loads[1].wait()
    turn(xl, 0)
    gather_b_z.send(3)
    gather_b_y.send(1, [3, 4])
    gather_a_y.finish()
    gather_a_z.send(1, [3])
    gather_a_z.send(2, [0])
    turn(xl, 1)
    gather_b_z.send(4)
    gather_b_y.send(1, [5, 6])
    gather_a_z.send(2, [1, 2])
    turn(xl, 2)
    gather_b_z.finish()
    gather_b_y.send(1, [7])
    gather_b_y.send(2, [0, 1, 2])
    gather_a_z.send(2, [3])
    turn(xl, 3)
    gather_a_z.send(3, [0, 1])
    theirs = x2.at[1 - xl, x_rows, :]
    landed(theirs, 1)
    sends.start(theirs, theirs, core_sems.at[0, 0], core_sems.at[1, 0], sibling)
    gather_a_z.send(3, [2, 3])
    gather_b_y.send(2, [3, 4])
    other_x = pl.ds(pl.multiple_of((1 - core) * (t // 2), 16), t // 2)
    rest = x2.at[1 - xl, other_x, :]
    pltpu.make_async_remote_copy(
        src_ref=rest, dst_ref=rest, send_sem=core_sems.at[0, 0], recv_sem=core_sems.at[1, 0],
        device_id=sibling, device_id_type=MESH,
    ).wait_recv()
    turn(1 - xl, 0)
    gather_a_z.send(4, [0, 1])
    turn(1 - xl, 1)
    gather_b_y.send(2, [5, 6])
    gather_a_z.send(4, [2, 3])
    turn(1 - xl, 2)
    gather_b_y.send(2, [7])
    turn(1 - xl, 3)
    landed(hg2.at[1 - xl], 2)
    landed(up2.at[1 - xl], 3)
    for copy in loads[2:]:
        copy.wait()
    gather_b_y.finish()

    def scale_of(block):
        return jnp.left_shift(1, exp_ref[xl * d.blocks + block]).astype(F32)

    def inverse_of(block):
        return jnp.right_shift(64, exp_ref[xl * d.blocks + block]).astype(F32) * (1.0 / 64.0)

    def signs_of(block):
        return (1 - 2 * bits[block : block + 1, :]).astype(F32)

    def gate_tile(w_part, g_part, base, start, width):
        columns = slice(start, start + width)
        gate = jnp.zeros((2 * t, width), F32)
        for place in range(d.ny):
            at = slice(place * d.yrows, (place + 1) * d.yrows)
            gate = gate + jnp.dot(
                x2[:, :, at].reshape(2 * t, d.yrows), w_part[place, :, columns],
                preferred_element_type=F32,
            )
        at = slice(base + start, base + start + width)
        grad = hg2[:, :, at].reshape(2 * t, width).astype(F32)
        up = up2[:, :, at].reshape(2 * t, width).astype(F32)
        s = jax.nn.sigmoid(gate)
        gate_grad = (grad * up * s * (1.0 + gate * (1.0 - s))).astype(BF16)
        g_part[:, columns] = gate_grad
        upg2[:, :, at] = (grad * gate * s).astype(BF16).reshape(2, t, width)
        for piece in range(width // BLOCK):
            block = (base + start) // BLOCK + piece
            flipped = gate_grad[:, piece * BLOCK : (piece + 1) * BLOCK].astype(F32) * signs_of(block)
            rotated = jnp.dot(flipped.astype(BF16), had[...], preferred_element_type=F32)
            rotated = rotated * (scale_of(block) * ROOT)
            top = rotated.astype(BF16)
            rest = (rotated - top.astype(F32)).astype(BF16)
            put = slice(block * BLOCK, (block + 1) * BLOCK)
            for replica in (0, 1):
                mine = slice(replica * t, (replica + 1) * t)
                turned[replica, 0:t, put] = top[mine]
                turned[replica, t : 2 * t, put] = rest[mine]

    def quantized(lhs, replica, columns):
        value = jnp.dot(lhs, turned[replica, :, columns], preferred_element_type=F32)
        return jnp.clip(value, -127.0, 127.0).astype(BF16).astype(F32)

    def order(j, ring):
        return ring.place((ring.half - lax.div(j + 1, 2)) * (2 * lax.rem(j, 2) - 1))

    def grads_a(low, high):
        @pl.loop(low, high)
        def _(j):
            at = pl.ds(z_rows(order(j, ring_z)), rb)
            total = 0.0
            for replica in (0, 1):
                lhs = xt[replica, :, at, :].reshape(d.ny * rb, 2 * t)
                total = total + quantized(lhs, replica, slice(0, d.cols_a))
            sa[:, at, :] = total.reshape(d.ny, rb, d.cols_a)

    def grads_b(low, high):
        @pl.loop(low * 2, high * 2)
        def _(j):
            place = order(lax.div(j, 2), ring_y)
            at = pl.ds(pl.multiple_of(lax.rem(j, 2) * (d.yrows // 2), 16), d.yrows // 2)
            total = 0.0
            for replica in (0, 1):
                total = total + quantized(xt[replica, place, at, :], replica, slice(d.cols_a, hf))
            sb[place, at, :] = total

    at_sub = lambda ref: lambda side, step, sub: ref.at[side, step, sub]
    at_rows = lambda ref: lambda side, step, sub: ref.at[side, step, pl.ds(d.row_subs[sub][0], d.row_subs[sub][1]), :]
    scatter_a_z = Scatter(
        ring_z, d.ny, along_z_of_y(sa, far_y), along_z_of_y(oa, far_y), at_sub(la_z), (ra_z_s, ra_z_r), sends
    )
    scatter_a_y = Scatter(ring_y, 2, along_y(sa), along_y(oa), at_rows(la_y), (ra_y_s, ra_y_r), sends)
    scatter_b_y = Scatter(
        ring_y, d.nz, along_y_of_z(sb, far_z), along_y_of_z(ob, far_z), at_sub(lb_y), (rb_y_s, rb_y_r), sends
    )
    scatter_b_z = Scatter(ring_z, 2, along_z(sb), along_z(ob), at_rows(lb_z), (rb_z_s, rb_z_r), sends)

    for start in range(0, d.cols_b, 2 * BLOCK):
        gate_tile(wb, g_b, d.cols_a, start, min(2 * BLOCK, d.cols_b - start))
    grads_b(0, 1)
    scatter_b_y.send(1)
    gather_a_z.finish()
    for start in range(0, d.cols_a, 2 * BLOCK):
        gate_tile(wa, g_a, 0, start, min(2 * BLOCK, d.cols_a - start))
    grads_a(0, 1)
    scatter_a_z.send(1)
    sends.start(upg2.at[1 - xl], ug_ref.at[:, here], x_sems.at[0, 4], x_sems.at[1, 4], partner)
    ug_ref[:, here] = upg2[xl]
    grads_a(1, 3)
    grads_b(1, 3)
    scatter_a_z.send(2)
    scatter_b_y.send(2, [0, 1, 2])

    def partial_tile(place):
        total = 0.0
        for w_part, g_part in ((wa, g_a), (wb, g_b)):
            total = total + lax.dot_general(
                g_part[...], w_part[place], (((1,), (1,)), ((), ())), preferred_element_type=F32
            )
        return total.reshape(8, t // 4, d.yrows)

    @pl.loop(0, d.ny)
    def _(place):
        part[:, :, pl.ds(pl.multiple_of(place * d.yrows, BLOCK), d.yrows)] = partial_tile(place)

    @pl.loop(0, 4)
    def _(q):
        core_out[q] = part[2 * q + 1 - core].astype(BF16)

    sends.start(core_out, core_in, core_sems.at[0, 1], core_sems.at[1, 1], sibling)

    def x_stage():
        pltpu.make_async_remote_copy(
            src_ref=core_in, dst_ref=core_in, send_sem=core_sems.at[0, 1], recv_sem=core_sems.at[1, 1],
            device_id=sibling, device_id_type=MESH,
        ).wait_recv()
        places = (
            (1 - xl) * 2 + xh, xl * 2 + (1 - xh), (1 - xl) * 2 + (1 - xh),
        )
        for index, q in enumerate(places):
            chip_out[index] = (part[2 * q + core] + core_in[q].astype(F32)).astype(BF16)
            sends.start(
                chip_out.at[index], chip_in.at[index], ip_sems.at[0, index], ip_sems.at[1, index], across[index]
            )

    grads_a(3, 5)
    scatter_a_z.send(3)
    scatter_b_y.send(2, [3, 4])
    x_stage()
    grads_b(3, 4)
    scatter_b_y.send(2, [5, 6, 7])
    grads_a(5, 8)
    scatter_b_y.finish([0])
    scatter_b_z.send(1)
    scatter_a_z.send(4, [0, 1])
    scatter_b_y.finish([1, 2])
    scatter_b_z.send(2)
    scatter_a_z.send(4, [2, 3])
    scatter_b_y.finish([3, 4])
    scatter_b_z.send(3)
    scatter_a_z.finish([0])
    scatter_a_y.send(1)
    scatter_b_y.finish([5, 6])
    scatter_b_z.send(4)
    scatter_a_z.finish([1, 2])
    scatter_a_y.send(2)
    scatter_b_y.finish([7])
    scatter_a_z.finish([3])

    def restore(source, base, columns):
        for piece in range(columns // BLOCK):
            block = base // BLOCK + piece
            value = source[y, pl.ds(z_rows(z), rb), piece * BLOCK : (piece + 1) * BLOCK] * inverse_of(block)
            total = 0.0
            for _ in range(3):
                top = value.astype(BF16)
                total = total + jnp.dot(top, had[...], preferred_element_type=F32)
                value = value - top.astype(F32)
            source[y, pl.ds(z_rows(z), rb), piece * BLOCK : (piece + 1) * BLOCK] = total * (signs_of(block) * ROOT)
        near = pl.ds(pl.multiple_of(z_rows(z) + xl * d.rows, 8), d.rows)
        far = pl.ds(pl.multiple_of(z_rows(z) + (1 - xl) * d.rows, 8), d.rows)
        columns_at = pl.ds(pl.multiple_of(xl * hf + base, BLOCK), columns)
        which = 0 if base == 0 else 1
        sends.start(
            source.at[y, far, :], wg_ref.at[:, columns_at], fin_sems.at[0, which], fin_sems.at[1, which], partner
        )
        wg_ref[:, columns_at] = source[y, near, :]

    scatter_a_y.finish()
    restore(sa, 0, d.cols_a)
    scatter_b_z.finish()
    restore(sb, d.cols_a, d.cols_b)

    mine = xl * 2 + xh
    total = part[2 * mine + core] + core_in[mine].astype(F32)
    for index in range(3):
        slot = chip_in.at[index]
        pltpu.make_async_remote_copy(
            src_ref=slot, dst_ref=slot, send_sem=ip_sems.at[0, index], recv_sem=ip_sems.at[1, index],
            device_id=across[index], device_id_type=MESH,
        ).wait_recv()
        total = total + slot[...].astype(F32)
    ig_ref[...] = total.astype(BF16)

    landed(ug_ref.at[:, there], 4)
    for which, base, columns in ((0, 0, d.cols_a), (1, d.cols_a, d.cols_b)):
        slot = wg_ref.at[:, pl.ds(pl.multiple_of((1 - xl) * hf + base, BLOCK), columns)]
        pltpu.make_async_remote_copy(
            src_ref=slot, dst_ref=slot, send_sem=fin_sems.at[0, which], recv_sem=fin_sems.at[1, which],
            device_id=partner, device_id_type=MESH,
        ).wait_recv()
    sends.drain()


def hand_over(a_ref, b_ref, c_ref, a_out, b_out, c_out):
    a_out[...] = a_ref[...]
    b_out[...] = b_ref[...]
    c_out[...] = c_ref[...]


def local(ny, nz, layer_input, gate_weight, up_value, hidden_grad, sign_bits, scale_exponent):
    tokens, depth = layer_input.shape
    rows, hidden = gate_weight.shape
    d = Dims(ny, nz, tokens, depth, rows, hidden)
    t, hf, rb = d.tokens, d.half, d.rb
    hy, hz = ny // 2, nz // 2
    vm = lambda shape, dtype: pltpu.VMEM(shape, dtype)
    sem = lambda *shape: pltpu.SemaphoreType.DMA(shape)
    pair = lambda *shape: [sem(*shape), sem(*shape)]
    scratch = [
        vm((rows, hidden), BF16), vm((8, BLOCK), jnp.int32),
        vm((2, t, depth), BF16), vm((2, ny, d.yrows, 2 * t), BF16),
        vm((2, t, hf), BF16), vm((2, t, hf), BF16), vm((2, t, hf), BF16),
        vm((d.pad, hf), BF16), vm((d.pad, hf), BF16),
        vm((ny, d.yrows, d.cols_a), BF16), vm((ny, d.yrows, d.cols_b), BF16),
        vm((2 * t, d.cols_a), BF16), vm((2 * t, d.cols_b), BF16),
        vm((2, 2 * t, hf), BF16), vm((BLOCK, BLOCK), BF16),
        vm((ny, d.yrows, d.cols_a), F32), vm((ny, d.yrows, d.cols_b), F32),
        vm((ny, d.yrows, d.cols_a), BF16), vm((ny, d.yrows, d.cols_b), BF16),
        vm((2, hz, ny, rb, d.cols_a), BF16), vm((2, hy, rb, d.cols_a), BF16),
        vm((2, hy, nz, rb, d.cols_b), BF16), vm((2, hz, rb, d.cols_b), BF16),
        vm((8, t // 4, depth), F32), vm((4, t // 4, depth), BF16), vm((4, t // 4, depth), BF16),
        vm((3, t // 4, depth), BF16), vm((3, t // 4, depth), BF16),
        sem(2, 5), sem(2, 2), sem(2, 3), sem(2, 2), sem(4 + d.blocks),
        *pair(2, hy, 2), *pair(2, hz, ny), *pair(2, hz, 2), *pair(2, hy, nz),
        *pair(2, hz, ny), *pair(2, hy, 2), *pair(2, hy, nz), *pair(2, hz, 2),
    ]
    whole = pl.BlockSpec(memory_space=pltpu.VMEM)
    anywhere = pl.BlockSpec(memory_space=pl.ANY)
    results = pl.pallas_call(
        functools.partial(kernel, d),
        out_shape=(
            jax.ShapeDtypeStruct((t // 4, depth), BF16),
            jax.ShapeDtypeStruct((t, hidden), BF16),
            jax.ShapeDtypeStruct((rows, hidden), F32),
        ),
        in_specs=[anywhere] * 5 + [pl.BlockSpec(memory_space=pltpu.SMEM)],
        out_specs=(whole,) * 3,
        scratch_shapes=scratch,
        compiler_params=pltpu.CompilerParams(
            collective_id=0, has_side_effects=True, vmem_limit_bytes=56 * 1024 * 1024
        ),
        name="gate_backward",
    )(layer_input, gate_weight, up_value, hidden_grad, sign_bits, scale_exponent)
    return pl.pallas_call(
        hand_over,
        out_shape=tuple(jax.ShapeDtypeStruct(r.shape, r.dtype) for r in results),
        in_specs=[whole] * 3,
        out_specs=(whole,) * 3,
        name="hand_over",
    )(*results)


def build(mesh, ny, nz):
    return jax.shard_map(
        functools.partial(local, ny, nz),
        mesh=mesh,
        in_specs=(P("dp", None), P("dp", "mp"), P("dp", "mp"), P("dp", "mp"), P("mp"), P("mp")),
        out_specs=(P(("dp", "mp"), None), P("dp", "mp"), P("dp", "mp")),
        check_vma=False,
    )


def solution(mesh):
    return build(mesh, 4, 8)
```

```python
import functools
import math

import jax
import jax.numpy as jnp
from jax import lax
from jax.experimental import pallas as pl
from jax.experimental.pallas import tpu as pltpu
from jax.sharding import PartitionSpec as P

F32 = jnp.float32
BF16 = jnp.bfloat16
MESH = pl.DeviceIdType.MESH
BLOCK = 128
ROOT = 1.0 / math.sqrt(128.0)


def up_to(value, unit):
    return -(-value // unit) * unit


class Dims:
    def __init__(self, ny, nz, tokens, depth, rows, hidden):
        self.ny, self.nz = ny, nz
        self.tokens, self.depth, self.rows, self.hidden = tokens, depth, rows, hidden
        self.half = hidden // 2
        self.blocks = self.half // BLOCK
        self.cols_a = (self.blocks * 3 // 7) * BLOCK
        self.cols_b = self.half - self.cols_a
        self.rb = 2 * rows
        self.yrows = nz * self.rb
        self.pad = up_to(rows, 16)
        cut = up_to(self.rb // 2, 16)
        self.row_subs = ((0, cut), (cut, self.rb - cut))


class Ring:
    def __init__(self, me, length, at):
        self.me, self.length, self.half = me, length, length // 2
        self.sides = (at(lax.rem(me + 1, length)), at(lax.rem(me + length - 1, length)))

    def place(self, offset):
        return lax.rem(self.me + offset + self.length, self.length)


class Sends:
    def __init__(self):
        self.open = []

    def start(self, src, dst, send_sem, recv_sem, device):
        copy = pltpu.make_async_remote_copy(
            src_ref=src, dst_ref=dst, send_sem=send_sem, recv_sem=recv_sem,
            device_id=device, device_id_type=MESH,
        )
        copy.start()
        self.open.append(copy)

    def drain(self):
        for copy in self.open:
            copy.wait_send()
        self.open = []


def went(side, sub, count):
    return sub % 2 == side


def nearest_first(length):
    half = length // 2
    return [0] + [sign * hops for hops in range(1, half) for sign in (1, -1)] + [half]


class Gather:
    def __init__(self, ring, count, ref, sems, sends):
        self.ring, self.count, self.ref = ring, count, ref
        self.send_sems, self.recv_sems = sems
        self.sends = sends

    def wait_one(self, side, step, sub):
        origin = self.ring.place(-step if side == 0 else step)
        here = self.ref(origin, sub)
        pltpu.make_async_remote_copy(
            src_ref=here, dst_ref=here,
            send_sem=self.send_sems.at[side, step - 1, sub],
            recv_sem=self.recv_sems.at[side, step - 1, sub],
            device_id=self.ring.sides[side], device_id_type=MESH,
        ).wait_recv()

    def send(self, step, subs=None):
        last = step == self.ring.half
        for sub in range(self.count) if subs is None else subs:
            for side in (0, 1):
                if step > 1:
                    self.wait_one(side, step - 1, sub)
                if last and not went(side, sub, self.count):
                    continue
                origin = self.ring.place(-(step - 1) if side == 0 else step - 1)
                here = self.ref(origin, sub)
                self.sends.start(
                    here, here,
                    self.send_sems.at[side, step - 1, sub],
                    self.recv_sems.at[side, step - 1, sub],
                    self.ring.sides[side],
                )

    def finish(self):
        for sub in range(self.count):
            for side in (0, 1):
                if went(side, sub, self.count):
                    self.wait_one(side, self.ring.half, sub)


class Scatter:
    def __init__(self, ring, count, own, out, landing, sems, sends):
        self.ring, self.count, self.own, self.out, self.landing = ring, count, own, out, landing
        self.send_sems, self.recv_sems = sems
        self.sends = sends

    def arrived(self, side, step, sub):
        return step < 1 or step > 1 or went(side, sub, self.count)

    def take(self, side, step, sub):
        here = self.landing(side, step - 1, sub)
        pltpu.make_async_remote_copy(
            src_ref=here, dst_ref=here,
            send_sem=self.send_sems.at[side, step - 1, sub],
            recv_sem=self.recv_sems.at[side, step - 1, sub],
            device_id=self.ring.sides[side], device_id_type=MESH,
        ).wait_recv()
        return here[...].astype(F32)

    def send(self, step, subs=None):
        far = self.ring.half + 1 - step
        for sub in range(self.count) if subs is None else subs:
            for side in (0, 1):
                if step == 1 and not went(side, sub, self.count):
                    continue
                target = self.ring.place(far if side == 0 else -far)
                total = self.own(target, sub)[...]
                if step > 1 and self.arrived(side, step - 1, sub):
                    total = total + self.take(side, step - 1, sub)
                out = self.out(target, sub)
                out[...] = total.astype(BF16)
                self.sends.start(
                    out, self.landing(side, step - 1, sub),
                    self.send_sems.at[side, step - 1, sub],
                    self.recv_sems.at[side, step - 1, sub],
                    self.ring.sides[side],
                )

    def finish(self, subs=None):
        for sub in range(self.count) if subs is None else subs:
            mine = self.own(self.ring.me, sub)
            total = mine[...]
            for side in (0, 1):
                if self.arrived(side, self.ring.half, sub):
                    total = total + self.take(side, self.ring.half, sub)
            mine[...] = total


def hadamard_signs():
    both = jnp.bitwise_and(
        lax.broadcasted_iota(jnp.int32, (BLOCK, BLOCK), 0),
        lax.broadcasted_iota(jnp.int32, (BLOCK, BLOCK), 1),
    )
    for shift in (4, 2, 1):
        both = jnp.bitwise_xor(both, jnp.right_shift(both, shift))
    return (1 - 2 * jnp.bitwise_and(both, 1)).astype(F32).astype(BF16)


def kernel(
    dims,
    x_ref, w_ref, up_ref, hg_ref, bits_ref, exp_ref,
    ig_ref, ug_ref, wg_ref,
    w_own, bits, x2, xt, hg2, up2, upg2, wsend, wrecv, early_b, wa, wb, g_a, g_b, turned, had,
    sa, sb, oa, ob, la_z, la_y, lb_y, lb_z,
    part, core_out, core_in, chip_out, chip_in,
    x_sems, core_sems, ip_sems, fin_sems, local_sems,
    ga_y_s, ga_y_r, ga_z_s, ga_z_r, gb_z_s, gb_z_r, gb_y_s, gb_y_r,
    ra_z_s, ra_z_r, ra_y_s, ra_y_r, rb_y_s, rb_y_r, rb_z_s, rb_z_r,
):
    d = dims
    t, hf, rb = d.tokens, d.half, d.rb
    dp, mp = lax.axis_index("dp"), lax.axis_index("mp")
    xl, yz = lax.rem(dp, 2), lax.div(dp, 2)
    z, y = lax.rem(yz, d.nz), lax.div(yz, d.nz)
    core, xh = lax.rem(mp, 2), lax.div(mp, 2)

    def device(y=y, z=z, xl=xl, xh=xh, core=core):
        return {"dp": (y * d.nz + z) * 2 + xl, "mp": xh * 2 + core}

    ring_y = Ring(y, d.ny, lambda place: device(y=place))
    ring_z = Ring(z, d.nz, lambda place: device(z=place))
    partner, sibling = device(xl=1 - xl), device(core=1 - core)
    across = (partner, device(xh=1 - xh), device(xl=1 - xl, xh=1 - xh))

    barrier = pltpu.get_barrier_semaphore()
    opposite = device(y=ring_y.place(2))
    others = ring_y.sides + (opposite,) + ring_z.sides + across + (sibling,)
    for other in others:
        pl.semaphore_signal(barrier, inc=1, device_id=other, device_id_type=MESH)

    sends = Sends()
    loads = []

    def load(src, dst):
        copy = pltpu.make_async_copy(src, dst, local_sems.at[len(loads)])
        copy.start()
        loads.append(copy)

    here = pl.ds(pl.multiple_of(xl * hf, BLOCK), hf)
    there = pl.ds(pl.multiple_of((1 - xl) * hf, BLOCK), hf)

    load(w_ref, w_own)
    load(x_ref, x2.at[xl])
    load(hg_ref.at[:, here], hg2.at[xl])
    load(up_ref.at[:, here], up2.at[xl])
    for block in range(d.blocks):
        at = pl.ds(pl.multiple_of(xl * hf + block * BLOCK, BLOCK), BLOCK)
        load(bits_ref.at[at], bits.at[block])

    def padded(columns):
        rows = w_own[:, columns].astype(F32)
        if d.pad == d.rows:
            return rows
        return jnp.concatenate([rows, jnp.zeros((d.pad - d.rows, hf), F32)], axis=0)

    loads[0].wait()
    wsend[...] = padded(there).astype(BF16)
    pl.semaphore_wait(barrier, len(others))

    for index, columns in ((0, slice(d.cols_a, hf)), (5, slice(0, d.cols_a))):
        sends.start(
            wsend.at[:, columns], wrecv.at[:, columns], x_sems.at[0, index], x_sems.at[1, index], partner
        )
    x_rows = pl.ds(pl.multiple_of(core * (t // 2), 16), t // 2)
    sends.start(x_ref.at[x_rows, :], x2.at[xl, x_rows, :], x_sems.at[0, 1], x_sems.at[1, 1], partner)
    sends.start(hg_ref.at[:, there], hg2.at[xl], x_sems.at[0, 2], x_sems.at[1, 2], partner)
    sends.start(up_ref.at[:, there], up2.at[xl], x_sems.at[0, 3], x_sems.at[1, 3], partner)

    def landed(ref, index):
        pltpu.make_async_remote_copy(
            src_ref=ref, dst_ref=ref, send_sem=x_sems.at[0, index], recv_sem=x_sems.at[1, index],
            device_id=partner, device_id_type=MESH,
        ).wait_recv()

    z_rows = lambda place: pl.multiple_of(place * rb, 16)
    near_y, near_z = nearest_first(d.ny), nearest_first(d.nz)
    far_y, far_z = near_y[::-1], near_z[::-1]
    part_of = lambda place, sub: pl.ds(z_rows(place) + d.row_subs[sub][0], d.row_subs[sub][1])

    def along_z(ref):
        return lambda place, sub: ref.at[y, part_of(place, sub), :]

    def along_z_of_y(ref, offsets):
        return lambda place, sub: ref.at[ring_y.place(offsets[sub]), pl.ds(z_rows(place), rb), :]

    def along_y_of_z(ref, offsets):
        return lambda place, sub: ref.at[place, pl.ds(z_rows(ring_z.place(offsets[sub])), rb), :]

    gather_a_z = Gather(ring_z, d.ny, along_z_of_y(wa, near_y), (ga_z_s, ga_z_r), sends)
    gather_b_z = Gather(ring_z, 2, along_z(wb), (gb_z_s, gb_z_r), sends)
    gather_b_y = Gather(ring_y, d.nz, along_y_of_z(wb, near_z), (gb_y_s, gb_y_r), sends)

    def assemble(index, columns, width, target):
        landed(wrecv.at[:, columns], index)
        own_at = pl.ds(pl.multiple_of(xl * hf + columns.start, BLOCK), width)
        own_rows = w_own[:, own_at].astype(F32)
        other_rows = wrecv[:, columns].astype(F32)[: d.rows]
        low = jnp.where(xl == 0, own_rows, other_rows)
        high = jnp.where(xl == 0, other_rows, own_rows)
        target[y, pl.ds(z_rows(z), rb), :] = jnp.concatenate([low, high], axis=0).astype(BF16)

    per_y = d.yrows // BLOCK

    def turn(replica, place):
        @pl.loop(0, per_y)
        def _(chunk):
            at = pl.ds(pl.multiple_of(chunk * BLOCK, BLOCK), BLOCK)
            tile = x2[replica, :, pl.ds(pl.multiple_of(place * d.yrows + chunk * BLOCK, BLOCK), BLOCK)]
            tile = tile.astype(F32).T.astype(BF16)
            xt[replica, place, at, 0:t] = tile
            xt[replica, place, at, t : 2 * t] = tile

    hops_y = (1, -1, 2)

    def block_a(place):
        return wa.at[place, pl.ds(z_rows(z), rb), :]

    def come_a(index):
        ref = block_a(ring_y.place(-hops_y[index]))
        pltpu.make_async_remote_copy(
            src_ref=ref, dst_ref=ref, send_sem=ga_y_s.at[index], recv_sem=ga_y_r.at[index],
            device_id=opposite, device_id_type=MESH,
        ).wait_recv()

    assemble(0, slice(d.cols_a, hf), d.cols_b, wb)
    gather_b_z.send(1)
    gather_b_y.send(1, [0])
    assemble(5, slice(0, d.cols_a), d.cols_a, wa)
    for index in (2, 0, 1):
        sends.start(
            block_a(y), block_a(y), ga_y_s.at[index], ga_y_r.at[index],
            device(y=ring_y.place(hops_y[index])),
        )
    gather_a_z.send(1, [0])
    had[...] = hadamard_signs()
    gather_b_z.send(2)
    gather_b_y.send(1, [1, 2])
    come_a(0)
    come_a(1)
    gather_a_z.send(1, [1, 2])
    loads[1].wait()
    turn(xl, 0)
    gather_b_z.send(3)
    gather_b_y.send(1, [3, 4])
    come_a(2)
    gather_a_z.send(1, [3])
    gather_a_z.send(2, [0])
    turn(xl, 1)
    gather_b_z.send(4)
    gather_b_y.send(1, [5, 6])
    gather_a_z.send(2, [1, 2])
    turn(xl, 2)
    gather_b_z.finish()
    gather_b_y.send(1, [7])
    gather_b_y.send(2, [0, 1, 2])
    gather_a_z.send(2, [3])
    turn(xl, 3)
    gather_a_z.send(3, [0, 1])
    theirs = x2.at[1 - xl, x_rows, :]
    landed(theirs, 1)
    sends.start(theirs, theirs, core_sems.at[0, 0], core_sems.at[1, 0], sibling)
    gather_a_z.send(3, [2, 3])
    gather_b_y.send(2, [3, 4])
    other_x = pl.ds(pl.multiple_of((1 - core) * (t // 2), 16), t // 2)
    rest = x2.at[1 - xl, other_x, :]
    pltpu.make_async_remote_copy(
        src_ref=rest, dst_ref=rest, send_sem=core_sems.at[0, 0], recv_sem=core_sems.at[1, 0],
        device_id=sibling, device_id_type=MESH,
    ).wait_recv()
    turn(1 - xl, 0)
    gather_a_z.send(4, [0, 1])
    turn(1 - xl, 1)
    gather_b_y.send(2, [5, 6])
    gather_a_z.send(4, [2, 3])
    turn(1 - xl, 2)
    gather_b_y.send(2, [7])
    turn(1 - xl, 3)
    landed(hg2.at[1 - xl], 2)
    landed(up2.at[1 - xl], 3)
    for copy in loads[2:]:
        copy.wait()

    def gate_sum(w_part, columns, places):
        total = 0.0
        for place in places:
            at = pl.ds(pl.multiple_of(place * d.yrows, BLOCK), d.yrows)
            total = total + jnp.dot(
                x2[:, :, at].reshape(2 * t, d.yrows), w_part[place, :, columns],
                preferred_element_type=F32,
            )
        return total

    tiles_b = [(start, min(2 * BLOCK, d.cols_b - start)) for start in range(0, d.cols_b, 2 * BLOCK)]
    tiles_a = [(start, min(2 * BLOCK, d.cols_a - start)) for start in range(0, d.cols_a, 2 * BLOCK)]
    early = [ring_y.place(hops) for hops in (0, 1, -1)]
    for start, width in tiles_b:
        early_b[:, start : start + width] = gate_sum(wb, slice(start, start + width), early)
    gather_b_y.finish()

    def scale_of(block):
        return jnp.left_shift(1, exp_ref[xl * d.blocks + block]).astype(F32)

    def inverse_of(block):
        return jnp.right_shift(64, exp_ref[xl * d.blocks + block]).astype(F32) * (1.0 / 64.0)

    def signs_of(block):
        return (1 - 2 * bits[block : block + 1, :]).astype(F32)

    def gate_tile(gate, g_part, base, start, width):
        columns = slice(start, start + width)
        at = slice(base + start, base + start + width)
        grad = hg2[:, :, at].reshape(2 * t, width).astype(F32)
        up = up2[:, :, at].reshape(2 * t, width).astype(F32)
        s = jax.nn.sigmoid(gate)
        gate_grad = (grad * up * s * (1.0 + gate * (1.0 - s))).astype(BF16)
        g_part[:, columns] = gate_grad
        upg2[:, :, at] = (grad * gate * s).astype(BF16).reshape(2, t, width)
        for piece in range(width // BLOCK):
            block = (base + start) // BLOCK + piece
            flipped = gate_grad[:, piece * BLOCK : (piece + 1) * BLOCK].astype(F32) * signs_of(block)
            rotated = jnp.dot(flipped.astype(BF16), had[...], preferred_element_type=F32)
            rotated = rotated * (scale_of(block) * ROOT)
            top = rotated.astype(BF16)
            rest = (rotated - top.astype(F32)).astype(BF16)
            put = slice(block * BLOCK, (block + 1) * BLOCK)
            for replica in (0, 1):
                mine = slice(replica * t, (replica + 1) * t)
                turned[replica, 0:t, put] = top[mine]
                turned[replica, t : 2 * t, put] = rest[mine]

    def quantized(lhs, replica, columns):
        value = jnp.dot(lhs, turned[replica, :, columns], preferred_element_type=F32)
        return jnp.clip(value, -127.0, 127.0).astype(BF16).astype(F32)

    def order(j, ring):
        return ring.place((ring.half - lax.div(j + 1, 2)) * (2 * lax.rem(j, 2) - 1))

    def grads_a(low, high):
        @pl.loop(low, high)
        def _(j):
            at = pl.ds(z_rows(order(j, ring_z)), rb)
            total = 0.0
            for replica in (0, 1):
                lhs = xt[replica, :, at, :].reshape(d.ny * rb, 2 * t)
                total = total + quantized(lhs, replica, slice(0, d.cols_a))
            sa[:, at, :] = total.reshape(d.ny, rb, d.cols_a)

    def grads_b(low, high):
        @pl.loop(low * 2, high * 2)
        def _(j):
            place = order(lax.div(j, 2), ring_y)
            at = pl.ds(pl.multiple_of(lax.rem(j, 2) * (d.yrows // 2), 16), d.yrows // 2)
            total = 0.0
            for replica in (0, 1):
                total = total + quantized(xt[replica, place, at, :], replica, slice(d.cols_a, hf))
            sb[place, at, :] = total

    at_sub = lambda ref: lambda side, step, sub: ref.at[side, step, sub]
    at_rows = lambda ref: lambda side, step, sub: ref.at[side, step, pl.ds(d.row_subs[sub][0], d.row_subs[sub][1]), :]
    scatter_a_z = Scatter(
        ring_z, d.ny, along_z_of_y(sa, far_y), along_z_of_y(oa, far_y), at_sub(la_z), (ra_z_s, ra_z_r), sends
    )
    scatter_b_y = Scatter(
        ring_y, d.nz, along_y_of_z(sb, far_z), along_y_of_z(ob, far_z), at_sub(lb_y), (rb_y_s, rb_y_r), sends
    )
    scatter_b_z = Scatter(ring_z, 2, along_z(sb), along_z(ob), at_rows(lb_z), (rb_z_s, rb_z_r), sends)

    for start, width in tiles_b:
        columns = slice(start, start + width)
        gate = early_b[:, columns] + gate_sum(wb, columns, [ring_y.place(2)])
        gate_tile(gate, g_b, d.cols_a, start, width)
    grads_b(0, 1)
    scatter_b_y.send(1)
    gather_a_z.finish()
    for start, width in tiles_a:
        gate_tile(gate_sum(wa, slice(start, start + width), range(d.ny)), g_a, 0, start, width)
    grads_a(0, 1)
    scatter_a_z.send(1)
    sends.start(upg2.at[1 - xl], ug_ref.at[:, here], x_sems.at[0, 4], x_sems.at[1, 4], partner)
    ug_ref[:, here] = upg2[xl]
    grads_a(1, 3)
    grads_b(1, 3)
    scatter_a_z.send(2)
    scatter_b_y.send(2, [0, 1, 2])

    def partial_tile(place):
        total = 0.0
        for w_part, g_part in ((wa, g_a), (wb, g_b)):
            total = total + lax.dot_general(
                g_part[...], w_part[place], (((1,), (1,)), ((), ())), preferred_element_type=F32
            )
        return total.reshape(8, t // 4, d.yrows)

    @pl.loop(0, d.ny)
    def _(place):
        part[:, :, pl.ds(pl.multiple_of(place * d.yrows, BLOCK), d.yrows)] = partial_tile(place)

    @pl.loop(0, 4)
    def _(q):
        core_out[q] = part[2 * q + 1 - core].astype(BF16)

    sends.start(core_out, core_in, core_sems.at[0, 1], core_sems.at[1, 1], sibling)

    def x_stage():
        pltpu.make_async_remote_copy(
            src_ref=core_in, dst_ref=core_in, send_sem=core_sems.at[0, 1], recv_sem=core_sems.at[1, 1],
            device_id=sibling, device_id_type=MESH,
        ).wait_recv()
        places = (
            (1 - xl) * 2 + xh, xl * 2 + (1 - xh), (1 - xl) * 2 + (1 - xh),
        )
        for index, q in enumerate(places):
            chip_out[index] = (part[2 * q + core] + core_in[q].astype(F32)).astype(BF16)
            sends.start(
                chip_out.at[index], chip_in.at[index], ip_sems.at[0, index], ip_sems.at[1, index], across[index]
            )

    grads_a(3, 5)
    scatter_a_z.send(3)
    scatter_b_y.send(2, [3, 4])
    x_stage()
    grads_b(3, 4)
    scatter_b_y.send(2, [5, 6, 7])
    grads_a(5, 8)
    scatter_b_y.finish([0])
    scatter_b_z.send(1)
    scatter_a_z.send(4, [0, 1])
    scatter_b_y.finish([1, 2])
    scatter_b_z.send(2)
    scatter_a_z.send(4, [2, 3])
    scatter_b_y.finish([3, 4])
    scatter_b_z.send(3)
    def pass_a(sub):
        scatter_a_z.finish([sub])
        index = hops_y.index({0: 2, 1: -1, 2: 1}[sub])
        target = ring_y.place(hops_y[index])
        at = pl.ds(z_rows(z), rb)
        oa[target, at, :] = sa[target, at, :].astype(BF16)
        sends.start(
            oa.at[target, at, :], la_y.at[index], ra_y_s.at[index], ra_y_r.at[index], device(y=target)
        )

    pass_a(0)
    scatter_b_y.finish([5, 6])
    scatter_b_z.send(4)
    pass_a(1)
    pass_a(2)
    scatter_b_y.finish([7])
    scatter_a_z.finish([3])

    def restore(source, base, columns):
        for piece in range(columns // BLOCK):
            block = base // BLOCK + piece
            value = source[y, pl.ds(z_rows(z), rb), piece * BLOCK : (piece + 1) * BLOCK] * inverse_of(block)
            total = 0.0
            for _ in range(3):
                top = value.astype(BF16)
                total = total + jnp.dot(top, had[...], preferred_element_type=F32)
                value = value - top.astype(F32)
            source[y, pl.ds(z_rows(z), rb), piece * BLOCK : (piece + 1) * BLOCK] = total * (signs_of(block) * ROOT)
        near = pl.ds(pl.multiple_of(z_rows(z) + xl * d.rows, 8), d.rows)
        far = pl.ds(pl.multiple_of(z_rows(z) + (1 - xl) * d.rows, 8), d.rows)
        columns_at = pl.ds(pl.multiple_of(xl * hf + base, BLOCK), columns)
        which = 0 if base == 0 else 1
        sends.start(
            source.at[y, far, :], wg_ref.at[:, columns_at], fin_sems.at[0, which], fin_sems.at[1, which], partner
        )
        wg_ref[:, columns_at] = source[y, near, :]

    own_a = sa[y, pl.ds(z_rows(z), rb), :]
    for index in (2, 0, 1):
        slot = la_y.at[index]
        pltpu.make_async_remote_copy(
            src_ref=slot, dst_ref=slot, send_sem=ra_y_s.at[index], recv_sem=ra_y_r.at[index],
            device_id=opposite, device_id_type=MESH,
        ).wait_recv()
        own_a = own_a + slot[...].astype(F32)
    sa[y, pl.ds(z_rows(z), rb), :] = own_a
    restore(sa, 0, d.cols_a)
    scatter_b_z.finish()
    restore(sb, d.cols_a, d.cols_b)

    mine = xl * 2 + xh
    total = part[2 * mine + core] + core_in[mine].astype(F32)
    for index in range(3):
        slot = chip_in.at[index]
        pltpu.make_async_remote_copy(
            src_ref=slot, dst_ref=slot, send_sem=ip_sems.at[0, index], recv_sem=ip_sems.at[1, index],
            device_id=across[index], device_id_type=MESH,
        ).wait_recv()
        total = total + slot[...].astype(F32)
    ig_ref[...] = total.astype(BF16)

    landed(ug_ref.at[:, there], 4)
    for which, base, columns in ((0, 0, d.cols_a), (1, d.cols_a, d.cols_b)):
        slot = wg_ref.at[:, pl.ds(pl.multiple_of((1 - xl) * hf + base, BLOCK), columns)]
        pltpu.make_async_remote_copy(
            src_ref=slot, dst_ref=slot, send_sem=fin_sems.at[0, which], recv_sem=fin_sems.at[1, which],
            device_id=partner, device_id_type=MESH,
        ).wait_recv()
    sends.drain()


def hand_over(a_ref, b_ref, c_ref, a_out, b_out, c_out):
    a_out[...] = a_ref[...]
    b_out[...] = b_ref[...]
    c_out[...] = c_ref[...]


def local(ny, nz, layer_input, gate_weight, up_value, hidden_grad, sign_bits, scale_exponent):
    tokens, depth = layer_input.shape
    rows, hidden = gate_weight.shape
    d = Dims(ny, nz, tokens, depth, rows, hidden)
    t, hf, rb = d.tokens, d.half, d.rb
    hy, hz = ny // 2, nz // 2
    vm = lambda shape, dtype: pltpu.VMEM(shape, dtype)
    sem = lambda *shape: pltpu.SemaphoreType.DMA(shape)
    pair = lambda *shape: [sem(*shape), sem(*shape)]
    scratch = [
        vm((rows, hidden), BF16), vm((8, BLOCK), jnp.int32),
        vm((2, t, depth), BF16), vm((2, ny, d.yrows, 2 * t), BF16),
        vm((2, t, hf), BF16), vm((2, t, hf), BF16), vm((2, t, hf), BF16),
        vm((d.pad, hf), BF16), vm((d.pad, hf), BF16),
        vm((2 * t, d.cols_b), F32),
        vm((ny, d.yrows, d.cols_a), BF16), vm((ny, d.yrows, d.cols_b), BF16),
        vm((2 * t, d.cols_a), BF16), vm((2 * t, d.cols_b), BF16),
        vm((2, 2 * t, hf), BF16), vm((BLOCK, BLOCK), BF16),
        vm((ny, d.yrows, d.cols_a), F32), vm((ny, d.yrows, d.cols_b), F32),
        vm((ny, d.yrows, d.cols_a), BF16), vm((ny, d.yrows, d.cols_b), BF16),
        vm((2, hz, ny, rb, d.cols_a), BF16), vm((3, rb, d.cols_a), BF16),
        vm((2, hy, nz, rb, d.cols_b), BF16), vm((2, hz, rb, d.cols_b), BF16),
        vm((8, t // 4, depth), F32), vm((4, t // 4, depth), BF16), vm((4, t // 4, depth), BF16),
        vm((3, t // 4, depth), BF16), vm((3, t // 4, depth), BF16),
        sem(2, 6), sem(2, 2), sem(2, 3), sem(2, 2), sem(4 + d.blocks),
        *pair(3), *pair(2, hz, ny), *pair(2, hz, 2), *pair(2, hy, nz),
        *pair(2, hz, ny), *pair(3), *pair(2, hy, nz), *pair(2, hz, 2),
    ]
    whole = pl.BlockSpec(memory_space=pltpu.VMEM)
    anywhere = pl.BlockSpec(memory_space=pl.ANY)
    results = pl.pallas_call(
        functools.partial(kernel, d),
        out_shape=(
            jax.ShapeDtypeStruct((t // 4, depth), BF16),
            jax.ShapeDtypeStruct((t, hidden), BF16),
            jax.ShapeDtypeStruct((rows, hidden), F32),
        ),
        in_specs=[anywhere] * 5 + [pl.BlockSpec(memory_space=pltpu.SMEM)],
        out_specs=(whole,) * 3,
        scratch_shapes=scratch,
        compiler_params=pltpu.CompilerParams(
            collective_id=0, has_side_effects=True, vmem_limit_bytes=56 * 1024 * 1024
        ),
        name="gate_backward",
    )(layer_input, gate_weight, up_value, hidden_grad, sign_bits, scale_exponent)
    return pl.pallas_call(
        hand_over,
        out_shape=tuple(jax.ShapeDtypeStruct(r.shape, r.dtype) for r in results),
        in_specs=[whole] * 3,
        out_specs=(whole,) * 3,
        name="hand_over",
    )(*results)


def build(mesh, ny, nz):
    return jax.shard_map(
        functools.partial(local, ny, nz),
        mesh=mesh,
        in_specs=(P("dp", None), P("dp", "mp"), P("dp", "mp"), P("dp", "mp"), P("mp"), P("mp")),
        out_specs=(P(("dp", "mp"), None), P("dp", "mp"), P("dp", "mp")),
        check_vma=False,
    )


def solution(mesh):
    return build(mesh, 4, 8)
```

```python
import functools
import math

import jax
import jax.numpy as jnp
from jax import lax
from jax.experimental import pallas as pl
from jax.experimental.pallas import tpu as pltpu
from jax.sharding import PartitionSpec as P

F32 = jnp.float32
BF16 = jnp.bfloat16
MESH = pl.DeviceIdType.MESH
BLOCK = 128
ROOT = 1.0 / math.sqrt(128.0)


def up_to(value, unit):
    return -(-value // unit) * unit


class Dims:
    def __init__(self, ny, nz, tokens, depth, rows, hidden):
        self.ny, self.nz = ny, nz
        self.tokens, self.depth, self.rows, self.hidden = tokens, depth, rows, hidden
        self.half = hidden // 2
        self.blocks = self.half // BLOCK
        self.cols_a = (self.blocks * 3 // 7) * BLOCK
        self.cols_b = self.half - self.cols_a
        self.rb = 2 * rows
        self.yrows = nz * self.rb
        self.pad = up_to(rows, 16)
        cut = up_to(self.rb // 2, 16)
        self.row_subs = ((0, cut), (cut, self.rb - cut))


class Ring:
    def __init__(self, me, length, at):
        self.me, self.length, self.half = me, length, length // 2
        self.sides = (at(lax.rem(me + 1, length)), at(lax.rem(me + length - 1, length)))

    def place(self, offset):
        return lax.rem(self.me + offset + self.length, self.length)


class Sends:
    def __init__(self):
        self.open = []

    def start(self, src, dst, send_sem, recv_sem, device):
        copy = pltpu.make_async_remote_copy(
            src_ref=src, dst_ref=dst, send_sem=send_sem, recv_sem=recv_sem,
            device_id=device, device_id_type=MESH,
        )
        copy.start()
        self.open.append(copy)

    def drain(self):
        for copy in self.open:
            copy.wait_send()
        self.open = []


def went(side, sub, count):
    return sub % 2 == side


def nearest_first(length):
    half = length // 2
    return [0] + [sign * hops for hops in range(1, half) for sign in (1, -1)] + [half]


class Gather:
    def __init__(self, ring, count, ref, sems, sends):
        self.ring, self.count, self.ref = ring, count, ref
        self.send_sems, self.recv_sems = sems
        self.sends = sends

    def wait_one(self, side, step, sub):
        origin = self.ring.place(-step if side == 0 else step)
        here = self.ref(origin, sub)
        pltpu.make_async_remote_copy(
            src_ref=here, dst_ref=here,
            send_sem=self.send_sems.at[side, step - 1, sub],
            recv_sem=self.recv_sems.at[side, step - 1, sub],
            device_id=self.ring.sides[side], device_id_type=MESH,
        ).wait_recv()

    def send(self, step, subs=None):
        last = step == self.ring.half
        for sub in range(self.count) if subs is None else subs:
            for side in (0, 1):
                if step > 1:
                    self.wait_one(side, step - 1, sub)
                if last and not went(side, sub, self.count):
                    continue
                origin = self.ring.place(-(step - 1) if side == 0 else step - 1)
                here = self.ref(origin, sub)
                self.sends.start(
                    here, here,
                    self.send_sems.at[side, step - 1, sub],
                    self.recv_sems.at[side, step - 1, sub],
                    self.ring.sides[side],
                )

    def finish(self):
        for sub in range(self.count):
            for side in (0, 1):
                if went(side, sub, self.count):
                    self.wait_one(side, self.ring.half, sub)


class Scatter:
    def __init__(self, ring, count, own, out, landing, sems, sends):
        self.ring, self.count, self.own, self.out, self.landing = ring, count, own, out, landing
        self.send_sems, self.recv_sems = sems
        self.sends = sends

    def arrived(self, side, step, sub):
        return step < 1 or step > 1 or went(side, sub, self.count)

    def take(self, side, step, sub):
        here = self.landing(side, step - 1, sub)
        pltpu.make_async_remote_copy(
            src_ref=here, dst_ref=here,
            send_sem=self.send_sems.at[side, step - 1, sub],
            recv_sem=self.recv_sems.at[side, step - 1, sub],
            device_id=self.ring.sides[side], device_id_type=MESH,
        ).wait_recv()
        return here[...].astype(F32)

    def send(self, step, subs=None):
        far = self.ring.half + 1 - step
        for sub in range(self.count) if subs is None else subs:
            for side in (0, 1):
                if step == 1 and not went(side, sub, self.count):
                    continue
                target = self.ring.place(far if side == 0 else -far)
                total = self.own(target, sub)[...]
                if step > 1 and self.arrived(side, step - 1, sub):
                    total = total + self.take(side, step - 1, sub)
                out = self.out(target, sub)
                out[...] = total.astype(BF16)
                self.sends.start(
                    out, self.landing(side, step - 1, sub),
                    self.send_sems.at[side, step - 1, sub],
                    self.recv_sems.at[side, step - 1, sub],
                    self.ring.sides[side],
                )

    def finish(self, subs=None):
        for sub in range(self.count) if subs is None else subs:
            mine = self.own(self.ring.me, sub)
            total = mine[...]
            for side in (0, 1):
                if self.arrived(side, self.ring.half, sub):
                    total = total + self.take(side, self.ring.half, sub)
            mine[...] = total


def hadamard_signs():
    both = jnp.bitwise_and(
        lax.broadcasted_iota(jnp.int32, (BLOCK, BLOCK), 0),
        lax.broadcasted_iota(jnp.int32, (BLOCK, BLOCK), 1),
    )
    for shift in (4, 2, 1):
        both = jnp.bitwise_xor(both, jnp.right_shift(both, shift))
    return (1 - 2 * jnp.bitwise_and(both, 1)).astype(F32).astype(BF16)


def kernel(
    dims,
    x_ref, w_ref, up_ref, hg_ref, bits_ref, exp_ref,
    ig_ref, ug_ref, wg_ref,
    w_own, bits, x2, xt, hg2, up2, upg2, wsend, wrecv, xz, early_a, early_b, wa, wb, g_a, g_b, turned, had,
    sa, sb, oa, ob, la_z, la_y, lb_y, lb_z,
    part, ig_own, core_out, core_in, chip_out, chip_in,
    x_sems, core_sems, ip_sems, fin_sems, local_sems, store_sems,
    ga_y_s, ga_y_r, ga_z_s, ga_z_r, gb_z_s, gb_z_r, gb_y_s, gb_y_r,
    ra_z_s, ra_z_r, ra_y_s, ra_y_r, rb_y_s, rb_y_r, rb_z_s, rb_z_r,
):
    d = dims
    t, hf, rb = d.tokens, d.half, d.rb
    dp, mp = lax.axis_index("dp"), lax.axis_index("mp")
    xl, yz = lax.rem(dp, 2), lax.div(dp, 2)
    z, y = lax.rem(yz, d.nz), lax.div(yz, d.nz)
    core, xh = lax.rem(mp, 2), lax.div(mp, 2)

    def device(y=y, z=z, xl=xl, xh=xh, core=core):
        return {"dp": (y * d.nz + z) * 2 + xl, "mp": xh * 2 + core}

    ring_y = Ring(y, d.ny, lambda place: device(y=place))
    ring_z = Ring(z, d.nz, lambda place: device(z=place))
    partner, sibling = device(xl=1 - xl), device(core=1 - core)
    across = (partner, device(xh=1 - xh), device(xl=1 - xl, xh=1 - xh))

    barrier = pltpu.get_barrier_semaphore()
    opposite = device(y=ring_y.place(2))
    others = ring_y.sides + (opposite,) + ring_z.sides + across + (sibling,)
    for other in others:
        pl.semaphore_signal(barrier, inc=1, device_id=other, device_id_type=MESH)

    sends = Sends()
    loads = []

    def load(src, dst):
        copy = pltpu.make_async_copy(src, dst, local_sems.at[len(loads)])
        copy.start()
        loads.append(copy)

    stores = []

    def store(src, dst):
        copy = pltpu.make_async_copy(src, dst, store_sems.at[len(stores)])
        copy.start()
        stores.append(copy)

    here = pl.ds(pl.multiple_of(xl * hf, BLOCK), hf)
    there = pl.ds(pl.multiple_of((1 - xl) * hf, BLOCK), hf)

    load(w_ref, w_own)
    load(x_ref, x2.at[xl])
    load(hg_ref.at[:, here], hg2.at[xl])
    load(up_ref.at[:, here], up2.at[xl])
    for block in range(d.blocks):
        at = pl.ds(pl.multiple_of(xl * hf + block * BLOCK, BLOCK), BLOCK)
        load(bits_ref.at[at], bits.at[block])

    def padded(columns):
        rows = w_own[:, columns].astype(F32)
        if d.pad == d.rows:
            return rows
        return jnp.concatenate([rows, jnp.zeros((d.pad - d.rows, hf), F32)], axis=0)

    loads[0].wait()
    wsend[...] = padded(there).astype(BF16)
    pl.semaphore_wait(barrier, len(others))

    for index, columns in ((0, slice(d.cols_a, hf)), (5, slice(0, d.cols_a))):
        sends.start(
            wsend.at[:, columns], wrecv.at[:, columns], x_sems.at[0, index], x_sems.at[1, index], partner
        )
    x_rows = pl.ds(pl.multiple_of(core * (t // 2), 16), t // 2)
    sends.start(x_ref.at[x_rows, :], x2.at[xl, x_rows, :], x_sems.at[0, 1], x_sems.at[1, 1], partner)
    sends.start(hg_ref.at[:, there], hg2.at[xl], x_sems.at[0, 2], x_sems.at[1, 2], partner)
    sends.start(up_ref.at[:, there], up2.at[xl], x_sems.at[0, 3], x_sems.at[1, 3], partner)

    def landed(ref, index):
        pltpu.make_async_remote_copy(
            src_ref=ref, dst_ref=ref, send_sem=x_sems.at[0, index], recv_sem=x_sems.at[1, index],
            device_id=partner, device_id_type=MESH,
        ).wait_recv()

    z_rows = lambda place: pl.multiple_of(place * rb, 16)
    near_y, near_z = nearest_first(d.ny), nearest_first(d.nz)
    far_y, far_z = near_y[::-1], near_z[::-1]
    part_of = lambda place, sub: pl.ds(z_rows(place) + d.row_subs[sub][0], d.row_subs[sub][1])

    def along_z(ref):
        return lambda place, sub: ref.at[y, part_of(place, sub), :]

    def along_z_of_y(ref, offsets):
        return lambda place, sub: ref.at[ring_y.place(offsets[sub]), pl.ds(z_rows(place), rb), :]

    def along_y_of_z(ref, offsets):
        return lambda place, sub: ref.at[place, pl.ds(z_rows(ring_z.place(offsets[sub])), rb), :]

    gather_a_z = Gather(ring_z, d.ny, along_z_of_y(wa, near_y), (ga_z_s, ga_z_r), sends)
    gather_b_z = Gather(ring_z, 2, along_z(wb), (gb_z_s, gb_z_r), sends)
    gather_b_y = Gather(ring_y, d.nz, along_y_of_z(wb, near_z), (gb_y_s, gb_y_r), sends)

    def assemble(index, columns, width, target):
        landed(wrecv.at[:, columns], index)
        own_at = pl.ds(pl.multiple_of(xl * hf + columns.start, BLOCK), width)
        own_rows = w_own[:, own_at].astype(F32)
        other_rows = wrecv[:, columns].astype(F32)[: d.rows]
        low = jnp.where(xl == 0, own_rows, other_rows)
        high = jnp.where(xl == 0, other_rows, own_rows)
        target[y, pl.ds(z_rows(z), rb), :] = jnp.concatenate([low, high], axis=0).astype(BF16)

    per_y = d.yrows // BLOCK

    def turn(replica, place):
        @pl.loop(0, per_y)
        def _(chunk):
            at = pl.ds(pl.multiple_of(chunk * BLOCK, BLOCK), BLOCK)
            tile = x2[replica, :, pl.ds(pl.multiple_of(place * d.yrows + chunk * BLOCK, BLOCK), BLOCK)]
            tile = tile.astype(F32).T.astype(BF16)
            xt[replica, place, at, 0:t] = tile
            xt[replica, place, at, t : 2 * t] = tile

    hops_y = (1, -1, 2)

    def block_a(place):
        return wa.at[place, pl.ds(z_rows(z), rb), :]

    def come_a(index):
        ref = block_a(ring_y.place(-hops_y[index]))
        pltpu.make_async_remote_copy(
            src_ref=ref, dst_ref=ref, send_sem=ga_y_s.at[index], recv_sem=ga_y_r.at[index],
            device_id=opposite, device_id_type=MESH,
        ).wait_recv()

    assemble(0, slice(d.cols_a, hf), d.cols_b, wb)
    def turn_z(replica):
        @pl.loop(0, d.nz)
        def _(place):
            tile = xt[replica, :, pl.ds(z_rows(place), rb), 0:t].reshape(d.ny * rb, t)
            at = pl.ds(pl.multiple_of(replica * t, BLOCK), t)
            xz[place, at, :] = tile.astype(F32).T.astype(BF16)

    gather_b_z.send(1)
    gather_b_y.send(1, [0])
    assemble(5, slice(0, d.cols_a), d.cols_a, wa)
    for index in (2, 0, 1):
        sends.start(
            block_a(y), block_a(y), ga_y_s.at[index], ga_y_r.at[index],
            device(y=ring_y.place(hops_y[index])),
        )
    gather_a_z.send(1, [0])
    had[...] = hadamard_signs()
    gather_b_z.send(2)
    gather_b_y.send(1, [1, 2])
    come_a(0)
    come_a(1)
    gather_a_z.send(1, [1, 2])
    loads[1].wait()
    turn(xl, 0)
    gather_b_z.send(3)
    gather_b_y.send(1, [3, 4])
    come_a(2)
    gather_a_z.send(1, [3])
    gather_a_z.send(2, [0])
    turn(xl, 1)
    gather_b_z.send(4)
    gather_b_y.send(1, [5, 6])
    gather_a_z.send(2, [1, 2])
    turn(xl, 2)
    gather_b_z.finish()
    gather_b_y.send(1, [7])
    gather_b_y.send(2, [0, 1, 2])
    gather_a_z.send(2, [3])
    turn(xl, 3)
    gather_a_z.send(3, [0, 1])
    turn_z(xl)
    theirs = x2.at[1 - xl, x_rows, :]
    landed(theirs, 1)
    sends.start(theirs, theirs, core_sems.at[0, 0], core_sems.at[1, 0], sibling)
    gather_a_z.send(3, [2, 3])
    gather_b_y.send(2, [3, 4])
    other_x = pl.ds(pl.multiple_of((1 - core) * (t // 2), 16), t // 2)
    rest = x2.at[1 - xl, other_x, :]
    pltpu.make_async_remote_copy(
        src_ref=rest, dst_ref=rest, send_sem=core_sems.at[0, 0], recv_sem=core_sems.at[1, 0],
        device_id=sibling, device_id_type=MESH,
    ).wait_recv()
    turn(1 - xl, 0)
    gather_a_z.send(4, [0, 1])
    turn(1 - xl, 1)
    gather_b_y.send(2, [5, 6])
    gather_a_z.send(4, [2, 3])
    turn(1 - xl, 2)
    gather_b_y.send(2, [7])
    turn(1 - xl, 3)
    turn_z(1 - xl)
    landed(hg2.at[1 - xl], 2)
    landed(up2.at[1 - xl], 3)
    for copy in loads[2:]:
        copy.wait()

    def gate_sum(w_part, columns, places):
        total = 0.0
        for place in places:
            at = pl.ds(pl.multiple_of(place * d.yrows, BLOCK), d.yrows)
            total = total + jnp.dot(
                x2[:, :, at].reshape(2 * t, d.yrows), w_part[place, :, columns],
                preferred_element_type=F32,
            )
        return total

    tiles_b = [(start, min(2 * BLOCK, d.cols_b - start)) for start in range(0, d.cols_b, 2 * BLOCK)]
    tiles_a = [(start, min(2 * BLOCK, d.cols_a - start)) for start in range(0, d.cols_a, 2 * BLOCK)]
    early = [ring_y.place(hops) for hops in (0, 1, -1)]
    def gate_sum_z(columns, places):
        total = 0.0
        for place in places:
            rows = wa[:, pl.ds(z_rows(place), rb), columns].reshape(d.ny * rb, columns.stop - columns.start)
            total = total + jnp.dot(xz[place], rows, preferred_element_type=F32)
        return total

    for start, width in tiles_a:
        columns = slice(start, start + width)
        early_a[:, columns] = gate_sum_z(columns, [ring_z.place(hops) for hops in near_z[:-1]])
    for start, width in tiles_b:
        early_b[:, start : start + width] = gate_sum(wb, slice(start, start + width), early)
    gather_a_z.finish()

    def scale_of(block):
        return jnp.left_shift(1, exp_ref[xl * d.blocks + block]).astype(F32)

    def inverse_of(block):
        return jnp.right_shift(64, exp_ref[xl * d.blocks + block]).astype(F32) * (1.0 / 64.0)

    def signs_of(block):
        return (1 - 2 * bits[block : block + 1, :]).astype(F32)

    def gate_tile(gate, g_part, base, start, width):
        columns = slice(start, start + width)
        at = slice(base + start, base + start + width)
        grad = hg2[:, :, at].reshape(2 * t, width).astype(F32)
        up = up2[:, :, at].reshape(2 * t, width).astype(F32)
        s = jax.nn.sigmoid(gate)
        gate_grad = (grad * up * s * (1.0 + gate * (1.0 - s))).astype(BF16)
        g_part[:, columns] = gate_grad
        upg2[:, :, at] = (grad * gate * s).astype(BF16).reshape(2, t, width)
        for piece in range(width // BLOCK):
            block = (base + start) // BLOCK + piece
            flipped = gate_grad[:, piece * BLOCK : (piece + 1) * BLOCK].astype(F32) * signs_of(block)
            rotated = jnp.dot(flipped.astype(BF16), had[...], preferred_element_type=F32)
            rotated = rotated * (scale_of(block) * ROOT)
            top = rotated.astype(BF16)
            rest = (rotated - top.astype(F32)).astype(BF16)
            put = slice(block * BLOCK, (block + 1) * BLOCK)
            for replica in (0, 1):
                mine = slice(replica * t, (replica + 1) * t)
                turned[replica, 0:t, put] = top[mine]
                turned[replica, t : 2 * t, put] = rest[mine]

    def quantized(lhs, replica, columns):
        value = jnp.dot(lhs, turned[replica, :, columns], preferred_element_type=F32)
        return jnp.clip(value, -127.0, 127.0).astype(BF16).astype(F32)

    def order(j, ring):
        return ring.place((ring.half - lax.div(j + 1, 2)) * (2 * lax.rem(j, 2) - 1))

    def grads_a(low, high):
        @pl.loop(low, high)
        def _(j):
            at = pl.ds(z_rows(order(j, ring_z)), rb)
            total = 0.0
            for replica in (0, 1):
                lhs = xt[replica, :, at, :].reshape(d.ny * rb, 2 * t)
                total = total + quantized(lhs, replica, slice(0, d.cols_a))
            sa[:, at, :] = total.reshape(d.ny, rb, d.cols_a)

    def grads_b(low, high):
        @pl.loop(low * 2, high * 2)
        def _(j):
            place = order(lax.div(j, 2), ring_y)
            at = pl.ds(pl.multiple_of(lax.rem(j, 2) * (d.yrows // 2), 16), d.yrows // 2)
            total = 0.0
            for replica in (0, 1):
                total = total + quantized(xt[replica, place, at, :], replica, slice(d.cols_a, hf))
            sb[place, at, :] = total

    at_sub = lambda ref: lambda side, step, sub: ref.at[side, step, sub]
    at_rows = lambda ref: lambda side, step, sub: ref.at[side, step, pl.ds(d.row_subs[sub][0], d.row_subs[sub][1]), :]
    scatter_a_z = Scatter(
        ring_z, d.ny, along_z_of_y(sa, far_y), along_z_of_y(oa, far_y), at_sub(la_z), (ra_z_s, ra_z_r), sends
    )
    scatter_b_y = Scatter(
        ring_y, d.nz, along_y_of_z(sb, far_z), along_y_of_z(ob, far_z), at_sub(lb_y), (rb_y_s, rb_y_r), sends
    )
    scatter_b_z = Scatter(ring_z, 2, along_z(sb), along_z(ob), at_rows(lb_z), (rb_z_s, rb_z_r), sends)

    for start, width in tiles_a:
        columns = slice(start, start + width)
        gate = early_a[:, columns] + gate_sum_z(columns, [ring_z.place(near_z[-1])])
        gate_tile(gate, g_a, 0, start, width)
    grads_a(0, 1)
    scatter_a_z.send(1)
    gather_b_y.finish()
    for start, width in tiles_b:
        columns = slice(start, start + width)
        gate = early_b[:, columns] + gate_sum(wb, columns, [ring_y.place(2)])
        gate_tile(gate, g_b, d.cols_a, start, width)
    grads_b(0, 1)
    scatter_b_y.send(1)
    sends.start(upg2.at[1 - xl], ug_ref.at[:, here], x_sems.at[0, 4], x_sems.at[1, 4], partner)
    store(upg2.at[xl], ug_ref.at[:, here])
    grads_a(1, 3)
    grads_b(1, 3)
    scatter_a_z.send(2)
    scatter_b_y.send(2, [0, 1, 2])

    def partial_tile(place):
        total = 0.0
        for w_part, g_part in ((wa, g_a), (wb, g_b)):
            total = total + lax.dot_general(
                g_part[...], w_part[place], (((1,), (1,)), ((), ())), preferred_element_type=F32
            )
        return total.reshape(8, t // 4, d.yrows)

    @pl.loop(0, d.ny)
    def _(place):
        part[:, :, pl.ds(pl.multiple_of(place * d.yrows, BLOCK), d.yrows)] = partial_tile(place)

    @pl.loop(0, 4)
    def _(q):
        core_out[q] = part[2 * q + 1 - core].astype(BF16)

    sends.start(core_out, core_in, core_sems.at[0, 1], core_sems.at[1, 1], sibling)

    def x_stage():
        pltpu.make_async_remote_copy(
            src_ref=core_in, dst_ref=core_in, send_sem=core_sems.at[0, 1], recv_sem=core_sems.at[1, 1],
            device_id=sibling, device_id_type=MESH,
        ).wait_recv()
        places = (
            (1 - xl) * 2 + xh, xl * 2 + (1 - xh), (1 - xl) * 2 + (1 - xh),
        )
        for index, q in enumerate(places):
            chip_out[index] = (part[2 * q + core] + core_in[q].astype(F32)).astype(BF16)
            sends.start(
                chip_out.at[index], chip_in.at[index], ip_sems.at[0, index], ip_sems.at[1, index], across[index]
            )

    grads_a(3, 5)
    scatter_a_z.send(3)
    scatter_b_y.send(2, [3, 4])
    x_stage()
    grads_b(3, 4)
    scatter_b_y.send(2, [5, 6, 7])
    grads_a(5, 8)
    scatter_b_y.finish([0])
    scatter_b_z.send(1)
    scatter_a_z.send(4, [0, 1])
    scatter_b_y.finish([1, 2])
    scatter_b_z.send(2)
    scatter_a_z.send(4, [2, 3])
    scatter_b_y.finish([3, 4])
    scatter_b_z.send(3)
    def pass_a(sub):
        scatter_a_z.finish([sub])
        index = hops_y.index({0: 2, 1: -1, 2: 1}[sub])
        target = ring_y.place(hops_y[index])
        at = pl.ds(z_rows(z), rb)
        oa[target, at, :] = sa[target, at, :].astype(BF16)
        sends.start(
            oa.at[target, at, :], la_y.at[index], ra_y_s.at[index], ra_y_r.at[index], device(y=target)
        )

    pass_a(0)
    scatter_b_y.finish([5, 6])
    scatter_b_z.send(4)
    pass_a(1)
    pass_a(2)

    mine = xl * 2 + xh
    total = part[2 * mine + core] + core_in[mine].astype(F32)
    for index in range(3):
        slot = chip_in.at[index]
        pltpu.make_async_remote_copy(
            src_ref=slot, dst_ref=slot, send_sem=ip_sems.at[0, index], recv_sem=ip_sems.at[1, index],
            device_id=across[index], device_id_type=MESH,
        ).wait_recv()
        total = total + slot[...].astype(F32)
    ig_own[...] = total.astype(BF16)
    store(ig_own, ig_ref)

    scatter_b_y.finish([7])
    scatter_a_z.finish([3])

    def restore(source, base, columns):
        for piece in range(columns // BLOCK):
            block = base // BLOCK + piece
            value = source[y, pl.ds(z_rows(z), rb), piece * BLOCK : (piece + 1) * BLOCK] * inverse_of(block)
            total = 0.0
            for _ in range(3):
                top = value.astype(BF16)
                total = total + jnp.dot(top, had[...], preferred_element_type=F32)
                value = value - top.astype(F32)
            source[y, pl.ds(z_rows(z), rb), piece * BLOCK : (piece + 1) * BLOCK] = total * (signs_of(block) * ROOT)
        near = pl.ds(pl.multiple_of(z_rows(z) + xl * d.rows, 8), d.rows)
        far = pl.ds(pl.multiple_of(z_rows(z) + (1 - xl) * d.rows, 8), d.rows)
        columns_at = pl.ds(pl.multiple_of(xl * hf + base, BLOCK), columns)
        which = 0 if base == 0 else 1
        sends.start(
            source.at[y, far, :], wg_ref.at[:, columns_at], fin_sems.at[0, which], fin_sems.at[1, which], partner
        )
        store(source.at[y, near, :], wg_ref.at[:, columns_at])

    own_a = sa[y, pl.ds(z_rows(z), rb), :]
    for index in (2, 0, 1):
        slot = la_y.at[index]
        pltpu.make_async_remote_copy(
            src_ref=slot, dst_ref=slot, send_sem=ra_y_s.at[index], recv_sem=ra_y_r.at[index],
            device_id=opposite, device_id_type=MESH,
        ).wait_recv()
        own_a = own_a + slot[...].astype(F32)
    sa[y, pl.ds(z_rows(z), rb), :] = own_a
    restore(sa, 0, d.cols_a)
    scatter_b_z.finish()
    restore(sb, d.cols_a, d.cols_b)

    landed(ug_ref.at[:, there], 4)
    for which, base, columns in ((0, 0, d.cols_a), (1, d.cols_a, d.cols_b)):
        slot = wg_ref.at[:, pl.ds(pl.multiple_of((1 - xl) * hf + base, BLOCK), columns)]
        pltpu.make_async_remote_copy(
            src_ref=slot, dst_ref=slot, send_sem=fin_sems.at[0, which], recv_sem=fin_sems.at[1, which],
            device_id=partner, device_id_type=MESH,
        ).wait_recv()
    for copy in stores:
        copy.wait()
    sends.drain()


def hand_over(a_ref, b_ref, c_ref, a_out, b_out, c_out, a_own, b_own, c_own, sems):
    moves = []
    for i, (src, own, dst) in enumerate(((c_ref, c_own, c_out), (a_ref, a_own, a_out), (b_ref, b_own, b_out))):
        moves.append((
            pltpu.make_async_copy(src, own, sems.at[0, i]), pltpu.make_async_copy(own, dst, sems.at[1, i])
        ))
    for into, _ in moves:
        into.start()
    for into, out in moves:
        into.wait()
        out.start()
    for _, out in moves:
        out.wait()


def local(ny, nz, layer_input, gate_weight, up_value, hidden_grad, sign_bits, scale_exponent):
    tokens, depth = layer_input.shape
    rows, hidden = gate_weight.shape
    d = Dims(ny, nz, tokens, depth, rows, hidden)
    t, hf, rb = d.tokens, d.half, d.rb
    hy, hz = ny // 2, nz // 2
    vm = lambda shape, dtype: pltpu.VMEM(shape, dtype)
    sem = lambda *shape: pltpu.SemaphoreType.DMA(shape)
    pair = lambda *shape: [sem(*shape), sem(*shape)]
    scratch = [
        vm((rows, hidden), BF16), vm((8, BLOCK), jnp.int32),
        vm((2, t, depth), BF16), vm((2, ny, d.yrows, 2 * t), BF16),
        vm((2, t, hf), BF16), vm((2, t, hf), BF16), vm((2, t, hf), BF16),
        vm((d.pad, hf), BF16), vm((d.pad, hf), BF16),
        vm((nz, 2 * t, ny * rb), BF16), vm((2 * t, d.cols_a), F32), vm((2 * t, d.cols_b), F32),
        vm((ny, d.yrows, d.cols_a), BF16), vm((ny, d.yrows, d.cols_b), BF16),
        vm((2 * t, d.cols_a), BF16), vm((2 * t, d.cols_b), BF16),
        vm((2, 2 * t, hf), BF16), vm((BLOCK, BLOCK), BF16),
        vm((ny, d.yrows, d.cols_a), F32), vm((ny, d.yrows, d.cols_b), F32),
        vm((ny, d.yrows, d.cols_a), BF16), vm((ny, d.yrows, d.cols_b), BF16),
        vm((2, hz, ny, rb, d.cols_a), BF16), vm((3, rb, d.cols_a), BF16),
        vm((2, hy, nz, rb, d.cols_b), BF16), vm((2, hz, rb, d.cols_b), BF16),
        vm((8, t // 4, depth), F32), vm((t // 4, depth), BF16), vm((4, t // 4, depth), BF16), vm((4, t // 4, depth), BF16),
        vm((3, t // 4, depth), BF16), vm((3, t // 4, depth), BF16),
        sem(2, 6), sem(2, 2), sem(2, 3), sem(2, 2), sem(4 + d.blocks), sem(4),
        *pair(3), *pair(2, hz, ny), *pair(2, hz, 2), *pair(2, hy, nz),
        *pair(2, hz, ny), *pair(3), *pair(2, hy, nz), *pair(2, hz, 2),
    ]
    hbm = pl.BlockSpec(memory_space=pltpu.HBM)
    anywhere = pl.BlockSpec(memory_space=pl.ANY)
    results = pl.pallas_call(
        functools.partial(kernel, d),
        out_shape=(
            jax.ShapeDtypeStruct((t // 4, depth), BF16),
            jax.ShapeDtypeStruct((t, hidden), BF16),
            jax.ShapeDtypeStruct((rows, hidden), F32),
        ),
        in_specs=[anywhere] * 5 + [pl.BlockSpec(memory_space=pltpu.SMEM)],
        out_specs=(hbm,) * 3,
        scratch_shapes=scratch,
        compiler_params=pltpu.CompilerParams(
            collective_id=0, has_side_effects=True, vmem_limit_bytes=56 * 1024 * 1024
        ),
        name="gate_backward",
    )(layer_input, gate_weight, up_value, hidden_grad, sign_bits, scale_exponent)
    return pl.pallas_call(
        hand_over,
        out_shape=tuple(jax.ShapeDtypeStruct(r.shape, r.dtype) for r in results),
        in_specs=[hbm] * 3,
        out_specs=(hbm,) * 3,
        scratch_shapes=[*(vm(r.shape, r.dtype) for r in results), sem(2, 3)],
        compiler_params=pltpu.CompilerParams(vmem_limit_bytes=60 * 1024 * 1024),
        name="hand_over",
    )(*results)


def build(mesh, ny, nz):
    return jax.shard_map(
        functools.partial(local, ny, nz),
        mesh=mesh,
        in_specs=(P("dp", None), P("dp", "mp"), P("dp", "mp"), P("dp", "mp"), P("mp"), P("mp")),
        out_specs=(P(("dp", "mp"), None), P("dp", "mp"), P("dp", "mp")),
        check_vma=False,
    )


def solution(mesh):
    return build(mesh, 4, 8)
```

```python
import functools
import math

import jax
import jax.numpy as jnp
from jax import lax
from jax.experimental import pallas as pl
from jax.experimental.pallas import tpu as pltpu
from jax.sharding import PartitionSpec as P

F32 = jnp.float32
BF16 = jnp.bfloat16
MESH = pl.DeviceIdType.MESH
BLOCK = 128
ROOT = 1.0 / math.sqrt(128.0)


def up_to(value, unit):
    return -(-value // unit) * unit


class Dims:
    def __init__(self, ny, nz, tokens, depth, rows, hidden):
        self.ny, self.nz = ny, nz
        self.tokens, self.depth, self.rows, self.hidden = tokens, depth, rows, hidden
        self.half = hidden // 2
        self.blocks = self.half // BLOCK
        self.cols_a = (self.blocks * 3 // 7) * BLOCK
        self.cols_b = self.half - self.cols_a
        self.rb = 2 * rows
        self.yrows = nz * self.rb
        self.pad = up_to(rows, 16)
        cut = up_to(self.rb // 2, 16)
        self.row_subs = ((0, cut), (cut, self.rb - cut))


class Ring:
    def __init__(self, me, length, at):
        self.me, self.length, self.half = me, length, length // 2
        self.sides = (at(lax.rem(me + 1, length)), at(lax.rem(me + length - 1, length)))

    def place(self, offset):
        return lax.rem(self.me + offset + self.length, self.length)


class Sends:
    def __init__(self):
        self.open = []

    def start(self, src, dst, send_sem, recv_sem, device):
        copy = pltpu.make_async_remote_copy(
            src_ref=src, dst_ref=dst, send_sem=send_sem, recv_sem=recv_sem,
            device_id=device, device_id_type=MESH,
        )
        copy.start()
        self.open.append(copy)

    def drain(self):
        for copy in self.open:
            copy.wait_send()
        self.open = []


def went(side, sub, count):
    return sub % 2 == side


def nearest_first(length):
    half = length // 2
    return [0] + [sign * hops for hops in range(1, half) for sign in (1, -1)] + [half]


class Gather:
    def __init__(self, ring, count, ref, sems, sends):
        self.ring, self.count, self.ref = ring, count, ref
        self.send_sems, self.recv_sems = sems
        self.sends = sends

    def wait_one(self, side, step, sub):
        origin = self.ring.place(-step if side == 0 else step)
        here = self.ref(origin, sub)
        pltpu.make_async_remote_copy(
            src_ref=here, dst_ref=here,
            send_sem=self.send_sems.at[side, step - 1, sub],
            recv_sem=self.recv_sems.at[side, step - 1, sub],
            device_id=self.ring.sides[side], device_id_type=MESH,
        ).wait_recv()

    def send(self, step, subs=None):
        last = step == self.ring.half
        for sub in range(self.count) if subs is None else subs:
            for side in (0, 1):
                if step > 1:
                    self.wait_one(side, step - 1, sub)
                if last and not went(side, sub, self.count):
                    continue
                origin = self.ring.place(-(step - 1) if side == 0 else step - 1)
                here = self.ref(origin, sub)
                self.sends.start(
                    here, here,
                    self.send_sems.at[side, step - 1, sub],
                    self.recv_sems.at[side, step - 1, sub],
                    self.ring.sides[side],
                )

    def finish(self):
        for sub in range(self.count):
            for side in (0, 1):
                if went(side, sub, self.count):
                    self.wait_one(side, self.ring.half, sub)


class Scatter:
    def __init__(self, ring, count, own, out, landing, sems, sends):
        self.ring, self.count, self.own, self.out, self.landing = ring, count, own, out, landing
        self.send_sems, self.recv_sems = sems
        self.sends = sends

    def arrived(self, side, step, sub):
        return step < 1 or step > 1 or went(side, sub, self.count)

    def take(self, side, step, sub):
        here = self.landing(side, step - 1, sub)
        pltpu.make_async_remote_copy(
            src_ref=here, dst_ref=here,
            send_sem=self.send_sems.at[side, step - 1, sub],
            recv_sem=self.recv_sems.at[side, step - 1, sub],
            device_id=self.ring.sides[side], device_id_type=MESH,
        ).wait_recv()
        return here[...].astype(F32)

    def send(self, step, subs=None):
        far = self.ring.half + 1 - step
        for sub in range(self.count) if subs is None else subs:
            for side in (0, 1):
                if step == 1 and not went(side, sub, self.count):
                    continue
                target = self.ring.place(far if side == 0 else -far)
                total = self.own(target, sub)[...]
                if step > 1 and self.arrived(side, step - 1, sub):
                    total = total + self.take(side, step - 1, sub)
                out = self.out(target, sub)
                out[...] = total.astype(BF16)
                self.sends.start(
                    out, self.landing(side, step - 1, sub),
                    self.send_sems.at[side, step - 1, sub],
                    self.recv_sems.at[side, step - 1, sub],
                    self.ring.sides[side],
                )

    def finish(self, subs=None):
        for sub in range(self.count) if subs is None else subs:
            mine = self.own(self.ring.me, sub)
            total = mine[...]
            for side in (0, 1):
                if self.arrived(side, self.ring.half, sub):
                    total = total + self.take(side, self.ring.half, sub)
            mine[...] = total


def hadamard_signs():
    both = jnp.bitwise_and(
        lax.broadcasted_iota(jnp.int32, (BLOCK, BLOCK), 0),
        lax.broadcasted_iota(jnp.int32, (BLOCK, BLOCK), 1),
    )
    for shift in (4, 2, 1):
        both = jnp.bitwise_xor(both, jnp.right_shift(both, shift))
    return (1 - 2 * jnp.bitwise_and(both, 1)).astype(F32).astype(BF16)


def kernel(
    dims,
    x_ref, w_ref, up_ref, hg_ref, bits_ref, exp_ref,
    ig_ref, ug_ref, wg_ref,
    w_own, bits, x2, xt, hg2, up2, upg2, wsend, wrecv, xz, early_a, early_b, wa, wb, g_a, g_b, turned, had,
    sa, sb, oa, ob, la_z, la_y, lb_y, lb_z,
    part, ig_own, core_out, core_in, chip_out, chip_in,
    x_sems, core_sems, ip_sems, fin_sems, local_sems, store_sems,
    ga_y_s, ga_y_r, ga_z_s, ga_z_r, gb_z_s, gb_z_r, gb_y_s, gb_y_r,
    ra_z_s, ra_z_r, ra_y_s, ra_y_r, rb_y_s, rb_y_r, rb_z_s, rb_z_r,
):
    d = dims
    t, hf, rb = d.tokens, d.half, d.rb
    dp, mp = lax.axis_index("dp"), lax.axis_index("mp")
    xl, yz = lax.rem(dp, 2), lax.div(dp, 2)
    z, y = lax.rem(yz, d.nz), lax.div(yz, d.nz)
    core, xh = lax.rem(mp, 2), lax.div(mp, 2)

    def device(y=y, z=z, xl=xl, xh=xh, core=core):
        return {"dp": (y * d.nz + z) * 2 + xl, "mp": xh * 2 + core}

    ring_y = Ring(y, d.ny, lambda place: device(y=place))
    ring_z = Ring(z, d.nz, lambda place: device(z=place))
    partner, sibling = device(xl=1 - xl), device(core=1 - core)
    across = (partner, device(xh=1 - xh), device(xl=1 - xl, xh=1 - xh))

    barrier = pltpu.get_barrier_semaphore()
    opposite = device(y=ring_y.place(2))
    others = ring_y.sides + (opposite,) + ring_z.sides + across + (sibling,)
    for other in others:
        pl.semaphore_signal(barrier, inc=1, device_id=other, device_id_type=MESH)

    sends = Sends()
    loads = []

    def load(src, dst):
        copy = pltpu.make_async_copy(src, dst, local_sems.at[len(loads)])
        copy.start()
        loads.append(copy)

    stores = []

    def store(src, dst):
        copy = pltpu.make_async_copy(src, dst, store_sems.at[len(stores)])
        copy.start()
        stores.append(copy)

    here = pl.ds(pl.multiple_of(xl * hf, BLOCK), hf)
    there = pl.ds(pl.multiple_of((1 - xl) * hf, BLOCK), hf)

    load(w_ref, w_own)
    load(x_ref, x2.at[xl])
    load(hg_ref.at[:, here], hg2.at[xl])
    load(up_ref.at[:, here], up2.at[xl])
    for block in range(d.blocks):
        at = pl.ds(pl.multiple_of(xl * hf + block * BLOCK, BLOCK), BLOCK)
        load(bits_ref.at[at], bits.at[block])

    def padded(columns):
        rows = w_own[:, columns].astype(F32)
        if d.pad == d.rows:
            return rows
        return jnp.concatenate([rows, jnp.zeros((d.pad - d.rows, hf), F32)], axis=0)

    loads[0].wait()
    wsend[...] = padded(there).astype(BF16)
    pl.semaphore_wait(barrier, len(others))

    for index, columns in ((0, slice(d.cols_a, hf)), (5, slice(0, d.cols_a))):
        sends.start(
            wsend.at[:, columns], wrecv.at[:, columns], x_sems.at[0, index], x_sems.at[1, index], partner
        )
    x_rows = pl.ds(pl.multiple_of(core * (t // 2), 16), t // 2)
    sends.start(x_ref.at[x_rows, :], x2.at[xl, x_rows, :], x_sems.at[0, 1], x_sems.at[1, 1], partner)
    sends.start(hg_ref.at[:, there], hg2.at[xl], x_sems.at[0, 2], x_sems.at[1, 2], partner)
    sends.start(up_ref.at[:, there], up2.at[xl], x_sems.at[0, 3], x_sems.at[1, 3], partner)

    def landed(ref, index):
        pltpu.make_async_remote_copy(
            src_ref=ref, dst_ref=ref, send_sem=x_sems.at[0, index], recv_sem=x_sems.at[1, index],
            device_id=partner, device_id_type=MESH,
        ).wait_recv()

    z_rows = lambda place: pl.multiple_of(place * rb, 16)
    near_y, near_z = nearest_first(d.ny), nearest_first(d.nz)
    far_y, far_z = near_y[::-1], near_z[::-1]
    part_of = lambda place, sub: pl.ds(z_rows(place) + d.row_subs[sub][0], d.row_subs[sub][1])

    def along_z(ref):
        return lambda place, sub: ref.at[y, part_of(place, sub), :]

    def along_z_of_y(ref, offsets):
        return lambda place, sub: ref.at[ring_y.place(offsets[sub]), pl.ds(z_rows(place), rb), :]

    def along_y_of_z(ref, offsets):
        return lambda place, sub: ref.at[place, pl.ds(z_rows(ring_z.place(offsets[sub])), rb), :]

    gather_a_z = Gather(ring_z, d.ny, along_z_of_y(wa, near_y), (ga_z_s, ga_z_r), sends)
    gather_b_z = Gather(ring_z, 2, along_z(wb), (gb_z_s, gb_z_r), sends)
    gather_b_y = Gather(ring_y, d.nz, along_y_of_z(wb, near_z), (gb_y_s, gb_y_r), sends)

    def assemble(index, columns, width, target):
        landed(wrecv.at[:, columns], index)
        own_at = pl.ds(pl.multiple_of(xl * hf + columns.start, BLOCK), width)
        own_rows = w_own[:, own_at].astype(F32)
        other_rows = wrecv[:, columns].astype(F32)[: d.rows]
        low = jnp.where(xl == 0, own_rows, other_rows)
        high = jnp.where(xl == 0, other_rows, own_rows)
        target[y, pl.ds(z_rows(z), rb), :] = jnp.concatenate([low, high], axis=0).astype(BF16)

    per_y = d.yrows // BLOCK

    def turn(replica, place):
        @pl.loop(0, per_y)
        def _(chunk):
            at = pl.ds(pl.multiple_of(chunk * BLOCK, BLOCK), BLOCK)
            tile = x2[replica, :, pl.ds(pl.multiple_of(place * d.yrows + chunk * BLOCK, BLOCK), BLOCK)]
            tile = tile.astype(F32).T.astype(BF16)
            xt[replica, place, at, 0:t] = tile
            xt[replica, place, at, t : 2 * t] = tile

    hops_y = (1, -1, 2)

    def block_a(place):
        return wa.at[place, pl.ds(z_rows(z), rb), :]

    def come_a(index):
        ref = block_a(ring_y.place(-hops_y[index]))
        pltpu.make_async_remote_copy(
            src_ref=ref, dst_ref=ref, send_sem=ga_y_s.at[index], recv_sem=ga_y_r.at[index],
            device_id=opposite, device_id_type=MESH,
        ).wait_recv()

    assemble(0, slice(d.cols_a, hf), d.cols_b, wb)
    def turn_z(replica):
        @pl.loop(0, d.nz)
        def _(place):
            tile = xt[replica, :, pl.ds(z_rows(place), rb), 0:t].reshape(d.ny * rb, t)
            at = pl.ds(pl.multiple_of(replica * t, BLOCK), t)
            xz[place, at, :] = tile.astype(F32).T.astype(BF16)

    gather_b_z.send(1)
    gather_b_y.send(1, [0])
    assemble(5, slice(0, d.cols_a), d.cols_a, wa)
    for index in (2, 0, 1):
        sends.start(
            block_a(y), block_a(y), ga_y_s.at[index], ga_y_r.at[index],
            device(y=ring_y.place(hops_y[index])),
        )
    gather_a_z.send(1, [0])
    had[...] = hadamard_signs()
    gather_b_z.send(2)
    gather_b_y.send(1, [1, 2])
    come_a(0)
    come_a(1)
    gather_a_z.send(1, [1, 2])
    loads[1].wait()
    turn(xl, 0)
    gather_b_z.send(3)
    gather_b_y.send(1, [3, 4])
    come_a(2)
    gather_a_z.send(1, [3])
    gather_a_z.send(2, [0])
    turn(xl, 1)
    gather_b_z.send(4)
    gather_b_y.send(1, [5, 6])
    gather_a_z.send(2, [1, 2])
    turn(xl, 2)
    gather_b_z.finish()
    gather_b_y.send(1, [7])
    gather_b_y.send(2, [0, 1, 2])
    gather_a_z.send(2, [3])
    turn(xl, 3)
    gather_a_z.send(3, [0, 1])
    turn_z(xl)
    theirs = x2.at[1 - xl, x_rows, :]
    landed(theirs, 1)
    sends.start(theirs, theirs, core_sems.at[0, 0], core_sems.at[1, 0], sibling)
    gather_a_z.send(3, [2, 3])
    gather_b_y.send(2, [3, 4])
    other_x = pl.ds(pl.multiple_of((1 - core) * (t // 2), 16), t // 2)
    rest = x2.at[1 - xl, other_x, :]
    pltpu.make_async_remote_copy(
        src_ref=rest, dst_ref=rest, send_sem=core_sems.at[0, 0], recv_sem=core_sems.at[1, 0],
        device_id=sibling, device_id_type=MESH,
    ).wait_recv()
    turn(1 - xl, 0)
    gather_a_z.send(4, [0, 1])
    turn(1 - xl, 1)
    gather_b_y.send(2, [5, 6])
    gather_a_z.send(4, [2, 3])
    turn(1 - xl, 2)
    gather_b_y.send(2, [7])
    turn(1 - xl, 3)
    turn_z(1 - xl)
    landed(hg2.at[1 - xl], 2)
    landed(up2.at[1 - xl], 3)
    for copy in loads[2:]:
        copy.wait()

    def gate_sum(w_part, columns, places):
        total = 0.0
        for place in places:
            at = pl.ds(pl.multiple_of(place * d.yrows, BLOCK), d.yrows)
            total = total + jnp.dot(
                x2[:, :, at].reshape(2 * t, d.yrows), w_part[place, :, columns],
                preferred_element_type=F32,
            )
        return total

    tiles_b = [(start, min(2 * BLOCK, d.cols_b - start)) for start in range(0, d.cols_b, 2 * BLOCK)]
    tiles_a = [(start, min(2 * BLOCK, d.cols_a - start)) for start in range(0, d.cols_a, 2 * BLOCK)]
    early = [ring_y.place(hops) for hops in (0, 1, -1)]
    def gate_sum_z(columns, places):
        total = 0.0
        for place in places:
            rows = wa[:, pl.ds(z_rows(place), rb), columns].reshape(d.ny * rb, columns.stop - columns.start)
            total = total + jnp.dot(xz[place], rows, preferred_element_type=F32)
        return total

    for start, width in tiles_a:
        columns = slice(start, start + width)
        early_a[:, columns] = gate_sum_z(columns, [ring_z.place(hops) for hops in near_z[:-1]])
    for start, width in tiles_b:
        early_b[:, start : start + width] = gate_sum(wb, slice(start, start + width), early)
    gather_a_z.finish()

    def scale_of(block):
        return jnp.left_shift(1, exp_ref[xl * d.blocks + block]).astype(F32)

    def inverse_of(block):
        return jnp.right_shift(64, exp_ref[xl * d.blocks + block]).astype(F32) * (1.0 / 64.0)

    def signs_of(block):
        return (1 - 2 * bits[block : block + 1, :]).astype(F32)

    def gate_tile(gate, g_part, base, start, width):
        columns = slice(start, start + width)
        at = slice(base + start, base + start + width)
        grad = hg2[:, :, at].reshape(2 * t, width).astype(F32)
        up = up2[:, :, at].reshape(2 * t, width).astype(F32)
        s = jax.nn.sigmoid(gate)
        gate_grad = (grad * up * s * (1.0 + gate * (1.0 - s))).astype(BF16)
        g_part[:, columns] = gate_grad
        upg2[:, :, at] = (grad * gate * s).astype(BF16).reshape(2, t, width)
        for piece in range(width // BLOCK):
            block = (base + start) // BLOCK + piece
            flipped = gate_grad[:, piece * BLOCK : (piece + 1) * BLOCK].astype(F32) * signs_of(block)
            rotated = jnp.dot(flipped.astype(BF16), had[...], preferred_element_type=F32)
            rotated = rotated * (scale_of(block) * ROOT)
            top = rotated.astype(BF16)
            rest = (rotated - top.astype(F32)).astype(BF16)
            put = slice(block * BLOCK, (block + 1) * BLOCK)
            for replica in (0, 1):
                mine = slice(replica * t, (replica + 1) * t)
                turned[replica, 0:t, put] = top[mine]
                turned[replica, t : 2 * t, put] = rest[mine]

    def quantized(lhs, replica, columns):
        value = jnp.dot(lhs, turned[replica, :, columns], preferred_element_type=F32)
        return jnp.clip(value, -127.0, 127.0).astype(BF16).astype(F32)

    def order(j, ring):
        return ring.place((ring.half - lax.div(j + 1, 2)) * (2 * lax.rem(j, 2) - 1))

    def grads_a(low, high):
        @pl.loop(low, high)
        def _(j):
            at = pl.ds(z_rows(order(j, ring_z)), rb)
            total = 0.0
            for replica in (0, 1):
                lhs = xt[replica, :, at, :].reshape(d.ny * rb, 2 * t)
                total = total + quantized(lhs, replica, slice(0, d.cols_a))
            sa[:, at, :] = total.reshape(d.ny, rb, d.cols_a)

    def grads_b(low, high):
        @pl.loop(low * 2, high * 2)
        def _(j):
            place = order(lax.div(j, 2), ring_y)
            at = pl.ds(pl.multiple_of(lax.rem(j, 2) * (d.yrows // 2), 16), d.yrows // 2)
            total = 0.0
            for replica in (0, 1):
                total = total + quantized(xt[replica, place, at, :], replica, slice(d.cols_a, hf))
            sb[place, at, :] = total

    at_sub = lambda ref: lambda side, step, sub: ref.at[side, step, sub]
    at_rows = lambda ref: lambda side, step, sub: ref.at[side, step, pl.ds(d.row_subs[sub][0], d.row_subs[sub][1]), :]
    scatter_a_z = Scatter(
        ring_z, d.ny, along_z_of_y(sa, far_y), along_z_of_y(oa, far_y), at_sub(la_z), (ra_z_s, ra_z_r), sends
    )
    scatter_b_y = Scatter(
        ring_y, d.nz, along_y_of_z(sb, far_z), along_y_of_z(ob, far_z), at_sub(lb_y), (rb_y_s, rb_y_r), sends
    )
    scatter_b_z = Scatter(ring_z, 2, along_z(sb), along_z(ob), at_rows(lb_z), (rb_z_s, rb_z_r), sends)

    for start, width in tiles_a:
        columns = slice(start, start + width)
        gate = early_a[:, columns] + gate_sum_z(columns, [ring_z.place(near_z[-1])])
        gate_tile(gate, g_a, 0, start, width)
    grads_a(0, 1)
    scatter_a_z.send(1)
    gather_b_y.finish()
    for start, width in tiles_b:
        columns = slice(start, start + width)
        gate = early_b[:, columns] + gate_sum(wb, columns, [ring_y.place(2)])
        gate_tile(gate, g_b, d.cols_a, start, width)
    grads_b(0, 1)
    scatter_b_y.send(1)
    sends.start(upg2.at[1 - xl], ug_ref.at[:, here], x_sems.at[0, 4], x_sems.at[1, 4], partner)
    store(upg2.at[xl], ug_ref.at[:, here])
    grads_a(1, 3)
    scatter_a_z.send(2)
    def partial_tile(place):
        total = 0.0
        for w_part, g_part in ((wa, g_a), (wb, g_b)):
            total = total + lax.dot_general(
                g_part[...], w_part[place], (((1,), (1,)), ((), ())), preferred_element_type=F32
            )
        return total.reshape(8, t // 4, d.yrows)

    @pl.loop(0, d.ny)
    def _(place):
        part[:, :, pl.ds(pl.multiple_of(place * d.yrows, BLOCK), d.yrows)] = partial_tile(place)

    @pl.loop(0, 4)
    def _(q):
        core_out[q] = part[2 * q + 1 - core].astype(BF16)

    sends.start(core_out, core_in, core_sems.at[0, 1], core_sems.at[1, 1], sibling)

    grads_b(1, 3)
    scatter_b_y.send(2, [0, 1, 2])

    def x_stage():
        pltpu.make_async_remote_copy(
            src_ref=core_in, dst_ref=core_in, send_sem=core_sems.at[0, 1], recv_sem=core_sems.at[1, 1],
            device_id=sibling, device_id_type=MESH,
        ).wait_recv()
        places = (
            (1 - xl) * 2 + xh, xl * 2 + (1 - xh), (1 - xl) * 2 + (1 - xh),
        )
        for index, q in enumerate(places):
            chip_out[index] = (part[2 * q + core] + core_in[q].astype(F32)).astype(BF16)
            sends.start(
                chip_out.at[index], chip_in.at[index], ip_sems.at[0, index], ip_sems.at[1, index], across[index]
            )

    grads_a(3, 5)
    scatter_a_z.send(3)
    scatter_b_y.send(2, [3, 4])
    x_stage()
    grads_b(3, 4)
    scatter_b_y.send(2, [5, 6, 7])
    grads_a(5, 8)
    scatter_b_y.finish([0])
    scatter_b_z.send(1)
    scatter_a_z.send(4, [0, 1])
    scatter_b_y.finish([1, 2])
    scatter_b_z.send(2)
    scatter_a_z.send(4, [2, 3])
    scatter_b_y.finish([3, 4])
    scatter_b_z.send(3)
    def pass_a(sub):
        scatter_a_z.finish([sub])
        index = hops_y.index({0: 2, 1: -1, 2: 1}[sub])
        target = ring_y.place(hops_y[index])
        at = pl.ds(z_rows(z), rb)
        oa[target, at, :] = sa[target, at, :].astype(BF16)
        sends.start(
            oa.at[target, at, :], la_y.at[index], ra_y_s.at[index], ra_y_r.at[index], device(y=target)
        )

    pass_a(0)
    scatter_b_y.finish([5, 6])
    scatter_b_z.send(4)
    pass_a(1)
    pass_a(2)

    mine = xl * 2 + xh
    total = part[2 * mine + core] + core_in[mine].astype(F32)
    for index in range(3):
        slot = chip_in.at[index]
        pltpu.make_async_remote_copy(
            src_ref=slot, dst_ref=slot, send_sem=ip_sems.at[0, index], recv_sem=ip_sems.at[1, index],
            device_id=across[index], device_id_type=MESH,
        ).wait_recv()
        total = total + slot[...].astype(F32)
    ig_own[...] = total.astype(BF16)
    store(ig_own, ig_ref)

    scatter_b_y.finish([7])
    scatter_a_z.finish([3])

    def restore(source, base, columns):
        for piece in range(columns // BLOCK):
            block = base // BLOCK + piece
            value = source[y, pl.ds(z_rows(z), rb), piece * BLOCK : (piece + 1) * BLOCK] * inverse_of(block)
            total = 0.0
            for _ in range(3):
                top = value.astype(BF16)
                total = total + jnp.dot(top, had[...], preferred_element_type=F32)
                value = value - top.astype(F32)
            source[y, pl.ds(z_rows(z), rb), piece * BLOCK : (piece + 1) * BLOCK] = total * (signs_of(block) * ROOT)
        near = pl.ds(pl.multiple_of(z_rows(z) + xl * d.rows, 8), d.rows)
        far = pl.ds(pl.multiple_of(z_rows(z) + (1 - xl) * d.rows, 8), d.rows)
        columns_at = pl.ds(pl.multiple_of(xl * hf + base, BLOCK), columns)
        which = 0 if base == 0 else 1
        sends.start(
            source.at[y, far, :], wg_ref.at[:, columns_at], fin_sems.at[0, which], fin_sems.at[1, which], partner
        )
        store(source.at[y, near, :], wg_ref.at[:, columns_at])

    own_a = sa[y, pl.ds(z_rows(z), rb), :]
    for index in (2, 0, 1):
        slot = la_y.at[index]
        pltpu.make_async_remote_copy(
            src_ref=slot, dst_ref=slot, send_sem=ra_y_s.at[index], recv_sem=ra_y_r.at[index],
            device_id=opposite, device_id_type=MESH,
        ).wait_recv()
        own_a = own_a + slot[...].astype(F32)
    sa[y, pl.ds(z_rows(z), rb), :] = own_a
    restore(sa, 0, d.cols_a)
    scatter_b_z.finish()
    restore(sb, d.cols_a, d.cols_b)

    landed(ug_ref.at[:, there], 4)
    for which, base, columns in ((0, 0, d.cols_a), (1, d.cols_a, d.cols_b)):
        slot = wg_ref.at[:, pl.ds(pl.multiple_of((1 - xl) * hf + base, BLOCK), columns)]
        pltpu.make_async_remote_copy(
            src_ref=slot, dst_ref=slot, send_sem=fin_sems.at[0, which], recv_sem=fin_sems.at[1, which],
            device_id=partner, device_id_type=MESH,
        ).wait_recv()
    for copy in stores:
        copy.wait()
    sends.drain()


def hand_over(a_ref, b_ref, c_ref, a_out, b_out, c_out, a_own, b_own, c_own, sems):
    moves = []
    for i, (src, own, dst) in enumerate(((c_ref, c_own, c_out), (a_ref, a_own, a_out), (b_ref, b_own, b_out))):
        moves.append((
            pltpu.make_async_copy(src, own, sems.at[0, i]), pltpu.make_async_copy(own, dst, sems.at[1, i])
        ))
    for into, _ in moves:
        into.start()
    for into, out in moves:
        into.wait()
        out.start()
    for _, out in moves:
        out.wait()


def local(ny, nz, layer_input, gate_weight, up_value, hidden_grad, sign_bits, scale_exponent):
    tokens, depth = layer_input.shape
    rows, hidden = gate_weight.shape
    d = Dims(ny, nz, tokens, depth, rows, hidden)
    t, hf, rb = d.tokens, d.half, d.rb
    hy, hz = ny // 2, nz // 2
    vm = lambda shape, dtype: pltpu.VMEM(shape, dtype)
    sem = lambda *shape: pltpu.SemaphoreType.DMA(shape)
    pair = lambda *shape: [sem(*shape), sem(*shape)]
    scratch = [
        vm((rows, hidden), BF16), vm((8, BLOCK), jnp.int32),
        vm((2, t, depth), BF16), vm((2, ny, d.yrows, 2 * t), BF16),
        vm((2, t, hf), BF16), vm((2, t, hf), BF16), vm((2, t, hf), BF16),
        vm((d.pad, hf), BF16), vm((d.pad, hf), BF16),
        vm((nz, 2 * t, ny * rb), BF16), vm((2 * t, d.cols_a), F32), vm((2 * t, d.cols_b), F32),
        vm((ny, d.yrows, d.cols_a), BF16), vm((ny, d.yrows, d.cols_b), BF16),
        vm((2 * t, d.cols_a), BF16), vm((2 * t, d.cols_b), BF16),
        vm((2, 2 * t, hf), BF16), vm((BLOCK, BLOCK), BF16),
        vm((ny, d.yrows, d.cols_a), F32), vm((ny, d.yrows, d.cols_b), F32),
        vm((ny, d.yrows, d.cols_a), BF16), vm((ny, d.yrows, d.cols_b), BF16),
        vm((2, hz, ny, rb, d.cols_a), BF16), vm((3, rb, d.cols_a), BF16),
        vm((2, hy, nz, rb, d.cols_b), BF16), vm((2, hz, rb, d.cols_b), BF16),
        vm((8, t // 4, depth), F32), vm((t // 4, depth), BF16), vm((4, t // 4, depth), BF16), vm((4, t // 4, depth), BF16),
        vm((3, t // 4, depth), BF16), vm((3, t // 4, depth), BF16),
        sem(2, 6), sem(2, 2), sem(2, 3), sem(2, 2), sem(4 + d.blocks), sem(4),
        *pair(3), *pair(2, hz, ny), *pair(2, hz, 2), *pair(2, hy, nz),
        *pair(2, hz, ny), *pair(3), *pair(2, hy, nz), *pair(2, hz, 2),
    ]
    hbm = pl.BlockSpec(memory_space=pltpu.HBM)
    anywhere = pl.BlockSpec(memory_space=pl.ANY)
    results = pl.pallas_call(
        functools.partial(kernel, d),
        out_shape=(
            jax.ShapeDtypeStruct((t // 4, depth), BF16),
            jax.ShapeDtypeStruct((t, hidden), BF16),
            jax.ShapeDtypeStruct((rows, hidden), F32),
        ),
        in_specs=[anywhere] * 5 + [pl.BlockSpec(memory_space=pltpu.SMEM)],
        out_specs=(hbm,) * 3,
        scratch_shapes=scratch,
        compiler_params=pltpu.CompilerParams(
            collective_id=0, has_side_effects=True, vmem_limit_bytes=56 * 1024 * 1024
        ),
        name="gate_backward",
    )(layer_input, gate_weight, up_value, hidden_grad, sign_bits, scale_exponent)
    return pl.pallas_call(
        hand_over,
        out_shape=tuple(jax.ShapeDtypeStruct(r.shape, r.dtype) for r in results),
        in_specs=[hbm] * 3,
        out_specs=(hbm,) * 3,
        scratch_shapes=[*(vm(r.shape, r.dtype) for r in results), sem(2, 3)],
        compiler_params=pltpu.CompilerParams(vmem_limit_bytes=60 * 1024 * 1024),
        name="hand_over",
    )(*results)


def build(mesh, ny, nz):
    return jax.shard_map(
        functools.partial(local, ny, nz),
        mesh=mesh,
        in_specs=(P("dp", None), P("dp", "mp"), P("dp", "mp"), P("dp", "mp"), P("mp"), P("mp")),
        out_specs=(P(("dp", "mp"), None), P("dp", "mp"), P("dp", "mp")),
        check_vma=False,
    )


def solution(mesh):
    return build(mesh, 4, 8)
```
